32 devices in a mesh: req: 8 (over z, x), tp: 4 (over y, core).
Axes of the slice: x: 2, y: 2, z: 4, core: 2. Of those that a mesh axis runs over, the one named last changes fastest.
Arguments:
- tokens: bfloat16 [2048, 1280], P('req'), as said below
- attention_gain: bfloat16 [1280], replicated, may hold values from 0.099609375 to 1.8984375
- feedforward_gain: bfloat16 [1280], replicated, may hold values from 0.099609375 to 1.8984375
- query_weight: bfloat16 [1280, 1280], P(None, 'tp'), may hold values from -0.15625 to 0.15625
- key_weight: bfloat16 [1280, 1280], P(None, 'tp'), may hold values from -0.625 to 0.625
- value_weight: bfloat16 [1280, 1280], P(None, 'tp'), may hold values from -0.3125 to 0.3125
- out_weight: bfloat16 [1280, 1280], P('tp'), may hold values from -0.3125 to 0.3125
- up_weight: bfloat16 [1280, 1280], P(None, 'tp'), may hold values from -0.15625 to 0.15625
- down_weight: bfloat16 [1280, 1280], P('tp'), may hold values from -0.15625 to 0.15625
- cache_keys: bfloat16 [8, 16, 192, 1280], P('req', None, None, 'tp'), as said below
- cache_values: bfloat16 [8, 16, 192, 1280], P('req', None, None, 'tp'), may hold values from -12 to 12
- request_prefix: int32 [16], replicated, may hold values from 0 to 15
- suffix_length: int32 [16], replicated, may hold values from 1 to 128, as said below
Outputs:
- layer_out: bfloat16 [2048, 1280], P('req', 'tp')
The draws below stay inside these ranges and needn't reach their ends.
Inputs may be any that keep to these rules, and one draw needn't show every extreme that they name: `suffix_length`: requests d * 2 to d * 2 + 1 are those of index d of req; their lengths sum to at most 192, on some index exactly 192; some request has exactly 128. `cache_keys`: keys of the cached prefix patches. `tokens`: patch embeddings.
All inputs are finite; a program needn't handle non-finite values.
Results may differ from the reference program's by a relative error of at most 0.0055.
The reference program's roundings to bfloat16 on the way (of `normed`, `attention`, `middle`, `normed_middle` and `hidden`) count: a program that leaves them out, or rounds other values in their place, can miss the bound.
Values may be sent and summed in bfloat16 or wider, within the bound.
A program may use at most 128 MiB of HBM per device.

```python
import math
import jax
import jax.numpy as jnp
import numpy as np
from jax import lax

D = 1280
HEADS = 16
HDIM = 80
FF = 1280
PREFIXES = 16
SLOT = 128
R_DEV = 2
PG = 192
REQUESTS = 16
ROWS = 2048
LIVE = 192


def draw_tokens(key, part):
    first, second = jax.random.split(key, 2)
    row_scale = jnp.exp(jax.random.uniform(first, (ROWS, 1), jnp.float32, math.log(0.3), math.log(3.0)))
    column_scale = jnp.exp(math.log(0.3) + math.log(10.0) * jnp.arange(D, dtype=jnp.float32) / D)
    base = jax.random.normal(second, (ROWS, D), jnp.float32)
    return (base * row_scale * column_scale[None, :]).astype(jnp.bfloat16)


def draw_cache_keys(key, part):
    shape = (REQUESTS // R_DEV, PREFIXES, PG, D)
    first = jax.random.fold_in(key, 0)
    return (4.0 * jax.random.normal(first, shape, jnp.float32)).astype(jnp.bfloat16)


def draw_suffix_length(key, part):
    owner_count = REQUESTS // R_DEV
    first, second, third = jax.random.split(key, 3)
    factor_one = jax.random.randint(first, (owner_count, R_DEV), 0, SLOT)
    factor_two = jax.random.randint(second, (owner_count, R_DEV), 0, SLOT)
    raw_length = 1 + factor_one * factor_two // SLOT
    ranks = jnp.arange(R_DEV, dtype=jnp.int32)

    def cap_step(used, column):
        raw_column, rank = column
        room = LIVE - used - (R_DEV - 1 - rank)
        taken = jnp.minimum(raw_column, room)
        return (used + taken, taken)
    _, taken_all = lax.scan(cap_step, jnp.zeros((owner_count,), jnp.int32), (raw_length.T, ranks))
    lengths = taken_all.T
    chosen = jax.random.randint(third, (), 0, owner_count)
    remainder = LIVE - SLOT
    even_part = remainder // (R_DEV - 1)
    extra = jnp.where(ranks == R_DEV - 1, remainder - even_part * (R_DEV - 1), 0)
    full_row = jnp.where(ranks == 0, SLOT, even_part + extra)
    selected = (jnp.arange(owner_count) == chosen)[:, None]
    lengths = jnp.where(selected, full_row[None, :], lengths)
    return lengths.reshape(-1).astype(jnp.int32)


def plant(values, rng, least, high):
    extent = values.shape
    place = [jax.random.randint(jax.random.fold_in(rng, axis), (), 0, extent[axis]) for axis in range(len(extent))]
    values = values.at[tuple(place)].set(least)
    longest = extent.index(max(extent))
    place[longest] = (place[longest] + 1) % extent[longest]
    return values.at[tuple(place)].set(high)


def level_of(rng, shape, cuts, least, high):
    loudness, own = 1.0, jax.random.fold_in(rng, 6)
    for dim, blocks in cuts:
        heights = jnp.exp(jax.random.uniform(jax.random.fold_in(own, dim), (blocks,), jnp.float32, least / len(cuts), high / len(cuts)))
        loudness = loudness * jnp.repeat(heights, shape[dim] // blocks).reshape([-1 if axis == dim else 1 for axis in range(len(shape))])
    return loudness


def rank_table(count, lean):
    loads = [(1 << 20) // math.isqrt(standing ** lean) + 1 for standing in range(1, count + 1)]
    deviation = 1 + sum(loads) // (1 << 30)
    return np.cumsum(np.array([max(1, weight // deviation) for weight in loads]))


def ranked(key, shape, amount, skew):
    table = rank_table(amount, skew)
    pick = jax.random.randint(jax.random.fold_in(key, 1), shape, 0, int(table[amount - 1]))
    rank = jnp.searchsorted(jnp.asarray(table, jnp.int32), pick, side="right")
    return jax.random.permutation(jax.random.fold_in(key, 2), amount)[rank].astype(jnp.int32)


def bell_draw(stream_key, extent, scale, bound, shards=(), held_as=jnp.bfloat16):
    array = jax.random.normal(stream_key, extent, jnp.float32) * scale
    if len(shards) > 0:
        array = level_of(stream_key, extent, shards, -0.22, 0.18) * array
    return jnp.clip(array, min=-bound, max=bound).astype(held_as)


def setup_inputs(seed: int = 0) -> dict:
    key_list = jax.random.split(jax.random.key(seed), 14)
    tokens = draw_tokens(jax.random.fold_in(key_list[13], 71), 0)
    attention_gain = jnp.clip(1.0 + 0.18 * jax.random.normal(key_list[1], (D,), jnp.float32), 0.099609375, 1.8984375).astype(jnp.bfloat16)
    feedforward_gain = jnp.clip(1.0 + 0.18 * jax.random.normal(key_list[2], (D,), jnp.float32), 0.099609375, 1.8984375).astype(jnp.bfloat16)
    query_weight = bell_draw(key_list[3], (D, D), D ** -0.5, 0.15625, ((1, 4),))
    key_weight = bell_draw(key_list[4], (D, D), (D // 16) ** -0.5, 0.625, ((1, 4),))
    value_weight = bell_draw(key_list[5], (D, D), (D // 4) ** -0.5, 0.3125, ((1, 4),))
    out_weight = bell_draw(key_list[6], (D, D), (D // 4) ** -0.5, 0.3125, ((0, 4),))
    up_weight = bell_draw(key_list[7], (D, FF), D ** -0.5, 0.15625, ((1, 4),))
    down_weight = bell_draw(key_list[8], (FF, D), FF ** -0.5, 0.15625, ((0, 4),))
    cache_keys = draw_cache_keys(jax.random.fold_in(key_list[13], 71), 0)
    cache_values = bell_draw(key_list[10], (REQUESTS // R_DEV, PREFIXES, PG, D), 2.0, 12.0, ((0, 8), (3, 4)))
    request_prefix = plant(ranked(key_list[11], (REQUESTS,), PREFIXES, 2), jax.random.fold_in(key_list[11], 3), 0, PREFIXES - 1).astype(jnp.int32)
    suffix_length = draw_suffix_length(jax.random.fold_in(key_list[13], 71), 0)
    return dict(tokens=tokens, attention_gain=attention_gain, feedforward_gain=feedforward_gain, query_weight=query_weight, key_weight=key_weight, value_weight=value_weight, out_weight=out_weight, up_weight=up_weight, down_weight=down_weight, cache_keys=cache_keys, cache_values=cache_values, request_prefix=request_prefix, suffix_length=suffix_length)


EPSILON = 1e-06
NEGATIVE = -1e+30

def normalize(values, gain):
    floats = values.astype(jnp.float32)
    mean_square = lax.optimization_barrier(jnp.mean(floats * floats, axis=-1, keepdims=True))
    return (floats * lax.rsqrt(mean_square + EPSILON) * gain.astype(jnp.float32)).astype(jnp.bfloat16)

def rounded(values):
    return lax.optimization_barrier(values.astype(jnp.bfloat16)).astype(jnp.float32)

def reference(tokens, attention_gain, feedforward_gain, query_weight, key_weight, value_weight, out_weight, up_weight, down_weight, cache_keys, cache_values, request_prefix, suffix_length):
    score_scale = 1.0 / math.sqrt(HDIM)
    normed = normalize(tokens, attention_gain)
    queries = jnp.dot(normed, query_weight, preferred_element_type=jnp.float32).astype(jnp.bfloat16)
    keys_own = jnp.dot(normed, key_weight, preferred_element_type=jnp.float32).astype(jnp.bfloat16)
    values_own = jnp.dot(normed, value_weight, preferred_element_type=jnp.float32).astype(jnp.bfloat16)
    query_slots = queries.astype(jnp.float32).reshape(REQUESTS, SLOT, HEADS, HDIM)
    key_slots = keys_own.astype(jnp.float32).reshape(REQUESTS, SLOT, HEADS, HDIM)
    value_slots = values_own.astype(jnp.float32).reshape(REQUESTS, SLOT, HEADS, HDIM)
    own_scores = jnp.einsum('rqhe,rkhe->rhqk', query_slots, key_slots) * score_scale
    causal = jnp.arange(SLOT)[:, None] >= jnp.arange(SLOT)[None, :]
    own_scores = jnp.where(causal[None, None], own_scores, NEGATIVE)
    own_top = lax.optimization_barrier(jnp.max(own_scores, axis=-1))
    own_weights = jnp.exp(own_scores - own_top[..., None])
    own_total = lax.optimization_barrier(jnp.sum(own_weights, axis=-1))
    own_numer = jnp.einsum('rhqk,rkhe->rhqe', rounded(own_weights), value_slots)

    def owner_step(carry, owner):
        row_peak, denominator, numerator = carry
        keys_owner = lax.dynamic_index_in_dim(cache_keys, owner, 0, keepdims=False)[request_prefix]
        values_owner = lax.dynamic_index_in_dim(cache_values, owner, 0, keepdims=False)[request_prefix]
        keys_owner = keys_owner.astype(jnp.float32).reshape(REQUESTS, PG, HEADS, HDIM)
        values_owner = values_owner.astype(jnp.float32).reshape(REQUESTS, PG, HEADS, HDIM)
        scores = jnp.einsum('rqhe,rkhe->rhqk', query_slots, keys_owner) * score_scale
        top_value = rounded(lax.optimization_barrier(jnp.max(scores, axis=-1)))
        weights = jnp.exp(scores - top_value[..., None])
        total_mass = lax.optimization_barrier(jnp.sum(weights, axis=-1))
        numer_owner = jnp.einsum('rhqk,rkhe->rhqe', rounded(weights), values_owner)
        share_rows = rounded(numer_owner / total_mass[..., None])
        owner_mass = rounded(total_mass)
        new_peak = jnp.maximum(row_peak, top_value)
        rescale = jnp.exp(row_peak - new_peak)
        factor = owner_mass * jnp.exp(top_value - new_peak)
        new_denominator = denominator * rescale + factor
        new_numerator = numerator * rescale[..., None] + factor[..., None] * share_rows
        return ((new_peak, new_denominator, new_numerator), None)
    owner_count = REQUESTS // R_DEV
    start = (own_top, own_total, own_numer)
    (row_peak, denominator, numerator), _ = lax.scan(owner_step, start, jnp.arange(owner_count, dtype=jnp.int32))
    attention = (numerator / denominator[..., None]).astype(jnp.bfloat16)
    attention = jnp.transpose(attention, (0, 2, 1, 3)).reshape(ROWS, D)
    projected = jnp.dot(attention, out_weight, preferred_element_type=jnp.float32)
    middle = (tokens.astype(jnp.float32) + projected).astype(jnp.bfloat16)
    normed_middle = normalize(middle, feedforward_gain)
    hidden = jax.nn.silu(jnp.dot(normed_middle, up_weight, preferred_element_type=jnp.float32)).astype(jnp.bfloat16)
    layer = middle.astype(jnp.float32) + jnp.dot(hidden, down_weight, preferred_element_type=jnp.float32)
    live_mask = (jnp.arange(SLOT)[None, :] < suffix_length[:, None]).reshape(ROWS)
    return jnp.where(live_mask[:, None], layer, 0.0).astype(jnp.bfloat16)
```

```python
import functools
import math

import jax
import jax.numpy as jnp
from jax import lax
from jax.experimental import pallas as pl
from jax.experimental.pallas import tpu as pltpu
from jax.sharding import PartitionSpec as P

HDIM = 80
SLOT = 128
R_DEV = 2
PG = 192
LOCAL_HEADS = 4
WIDTH = HDIM * LOCAL_HEADS
ROWS = R_DEV * SLOT
STATS = 16
HALF = WIDTH // 2

EPSILON = 1e-06
NEGATIVE = -1e30
MESH = pl.DeviceIdType.MESH
F32 = jnp.float32
BF16 = jnp.bfloat16


def normalize(floats, gain):
    mean_square = jnp.mean(floats * floats, axis=-1, keepdims=True)
    return (floats * lax.rsqrt(mean_square + EPSILON) * gain).astype(BF16)


def matmul(left, right):
    return jnp.dot(left, right, preferred_element_type=F32)


def head_rows(values, head):
    return values[head * HDIM : (head + 1) * HDIM]


def request_partial(query_t, keys, values_t, causal):
    none = jnp.zeros((HDIM, SLOT), BF16)
    spread = jnp.concatenate(
        [
            jnp.concatenate(
                [head_rows(query_t, h) if g == h else none for g in range(LOCAL_HEADS)], axis=1
            )
            for h in range(LOCAL_HEADS)
        ],
        axis=0,
    )
    scores = matmul(keys, spread) * (1.0 / math.sqrt(HDIM))
    if causal:
        key_row = lax.broadcasted_iota(jnp.int32, scores.shape, 0)
        query_row = lax.broadcasted_iota(jnp.int32, scores.shape, 1) % SLOT
        scores = jnp.where(key_row <= query_row, scores, NEGATIVE)
    top = jnp.max(scores, axis=0, keepdims=True)
    if not causal:
        top = top.astype(BF16).astype(F32)
    weights = jnp.exp(scores - top)
    total = jnp.sum(weights, axis=0, keepdims=True)
    numer = matmul(values_t, weights.astype(BF16))
    lanes = [slice(h * SLOT, (h + 1) * SLOT) for h in range(LOCAL_HEADS)]
    return [(head_rows(numer, h)[:, lanes[h]], top[:, lanes[h]], total[:, lanes[h]]) for h in range(LOCAL_HEADS)]


def both_requests(first, second):
    return [
        tuple(jnp.concatenate([a, b], axis=1) for a, b in zip(first[h], second[h]))
        for h in range(LOCAL_HEADS)
    ]


def merge(one, other):
    merged = []
    for (numer_a, top_a, total_a), (numer_b, top_b, total_b) in zip(one, other):
        top = jnp.maximum(top_a, top_b)
        factor_a = jnp.exp(top_a - top)
        factor_b = jnp.exp(top_b - top)
        merged.append(
            (
                numer_a * factor_a + numer_b * factor_b,
                top,
                total_a * factor_a + total_b * factor_b,
            )
        )
    return merged


def pack_partial(partial):
    shares = [(numer / total).astype(BF16) for numer, _, total in partial]
    tops = [top for _, top, _ in partial]
    whole = [total.astype(BF16).astype(F32) for _, _, total in partial]
    rest = [total - high for (_, _, total), high in zip(partial, whole)]
    pad = [jnp.zeros((STATS - 3 * LOCAL_HEADS, ROWS), F32)]
    stats = jnp.concatenate(tops + whole + rest + pad, axis=0).astype(BF16)
    return jnp.concatenate(shares + [stats], axis=0)


def unpack_partial(block):
    stats = block[WIDTH:].astype(F32)
    partial = []
    for h in range(LOCAL_HEADS):
        top = stats[h : h + 1]
        total = stats[LOCAL_HEADS + h : LOCAL_HEADS + h + 1]
        total = total + stats[2 * LOCAL_HEADS + h : 2 * LOCAL_HEADS + h + 1]
        partial.append((head_rows(block, h).astype(F32) * total, top, total))
    return partial


def kernel(
    nz,
    tokens,
    gain_a,
    gain_f,
    wq,
    wk,
    wv,
    wo,
    wup,
    wdown,
    cache_k,
    cache_v,
    prefix,
    length,
    out,
    qbuf,
    kbuf,
    vbuf,
    wo_all,
    up_v,
    down_v,
    down_t,
    own_k,
    own_v,
    upward,
    downward,
    cross,
    att,
    core_out,
    core_in,
    y_out,
    y_in,
    mid_t,
    local_sem,
    qsend,
    qrecv,
    psend,
    precv,
    xsend,
    xrecv,
    tsend,
    trecv,
):
    me = lax.axis_index("req")
    tp = lax.axis_index("tp")
    z = me // 2
    x = me % 2
    mate = z * 2 + 1 - x
    core_mate = tp + 1 - 2 * (tp % 2)
    y_mate = (tp + 2) % 4
    not_first = z > 0
    not_last = z < nz - 1

    def remote(source, target, send_sem, recv_sem, **where):
        return pltpu.make_async_remote_copy(
            src_ref=source,
            dst_ref=target,
            send_sem=send_sem,
            recv_sem=recv_sem,
            device_id=where,
            device_id_type=MESH,
        )

    barrier = pltpu.get_barrier_semaphore()

    def greet(**where):
        pl.semaphore_signal(barrier, inc=1, device_id=where, device_id_type=MESH)

    greet(req=mate)
    greet(tp=core_mate)
    greet(tp=y_mate)
    pl.when(not_first)(lambda: greet(req=me - 2))
    pl.when(not_last)(lambda: greet(req=me + 2))

    loads = [
        pltpu.make_async_copy(source, target, local_sem.at[i])
        for i, (source, target) in enumerate(
            [(wo, wo_all.at[tp]), (cache_k, kbuf), (cache_v, vbuf), (wdown, down_v), (wup, up_v)]
        )
    ]
    for load in loads:
        load.start()

    normed = normalize(tokens[...].astype(F32), gain_a[...].astype(F32))
    qbuf[me] = matmul(normed, wq[...]).T.astype(BF16)

    pl.semaphore_wait(barrier, 3 + jnp.where(not_first, 1, 0) + jnp.where(not_last, 1, 0))

    def whole(plane, column):
        return qbuf.at[plane * 2 + column]

    def early(plane, column):
        return qbuf.at[plane * 2 + column, pl.ds(0, HALF)]

    def late(plane, column):
        return qbuf.at[plane * 2 + column, pl.ds(HALF, HALF)]

    def up_whole(plane):
        return remote(whole(plane, x), whole(plane, x), qsend.at[0, plane], qrecv.at[0, plane], req=me + 2)

    def up_early(plane):
        return remote(early(plane, 1 - x), early(plane, 1 - x), qsend.at[1, plane], qrecv.at[1, plane], req=me + 2)

    def down_whole(plane):
        return remote(whole(plane, x), whole(plane, x), qsend.at[2, plane], qrecv.at[0, plane], req=me - 2)

    def down_early(plane):
        return remote(early(plane, 1 - x), early(plane, 1 - x), qsend.at[3, plane], qrecv.at[1, plane], req=me - 2)

    def over_late(plane):
        return remote(late(plane, x), late(plane, x), qsend.at[4, plane], qrecv.at[2, plane], req=mate)

    over_whole = remote(whole(z, x), whole(z, x), qsend.at[4, z], qrecv.at[2, z], req=mate)
    got_whole = remote(whole(z, 1 - x), whole(z, 1 - x), qsend.at[4, z], qrecv.at[2, z], req=mate)

    over_whole.start()
    pl.when(not_last)(lambda: up_whole(z).start())
    pl.when(not_first)(lambda: down_whole(z).start())

    loads[0].wait()
    wo_y = remote(wo_all.at[tp], wo_all.at[tp], tsend.at[0], trecv.at[0], tp=y_mate)
    wo_core = remote(wo_all.at[tp], wo_all.at[tp], tsend.at[1], trecv.at[1], tp=core_mate)
    wo_y.start()
    wo_core.start()

    got_whole.wait_recv()
    pl.when(not_last)(lambda: up_early(z).start())
    pl.when(not_first)(lambda: down_early(z).start())

    own_k[...] = matmul(normed, wk[...]).astype(BF16)
    own_v[...] = matmul(normed, wv[...]).T.astype(BF16)
    loads[3].wait()
    down_t[...] = down_v[...].astype(F32).T.astype(BF16)

    def gather_step(step, carry):
        below = z - 1 - step
        above = z + 1 + step

        @pl.when(below >= 0)
        def _():
            up_whole(below).wait_recv()
            pl.when(not_last)(lambda: up_whole(below).start())
            over_late(below).start()

        @pl.when(above < nz)
        def _():
            down_whole(above).wait_recv()
            pl.when(not_first)(lambda: down_whole(above).start())
            over_late(above).start()

        @pl.when(below >= 0)
        def _():
            up_early(below).wait_recv()
            pl.when(not_last)(lambda: up_early(below).start())

        @pl.when(above < nz)
        def _():
            down_early(above).wait_recv()
            pl.when(not_first)(lambda: down_early(above).start())

        return carry

    lax.fori_loop(0, nz - 1, gather_step, 0)

    def late_step(plane, carry):
        @pl.when(plane != z)
        def _():
            remote(late(plane, 1 - x), late(plane, 1 - x), qsend.at[4, plane], qrecv.at[2, plane], req=mate).wait_recv()

        return carry

    lax.fori_loop(0, nz, late_step, 0)
    loads[1].wait()
    loads[2].wait()

    def cached(target):
        queries = qbuf[target]
        parts = []
        for j in range(R_DEV):
            chosen = prefix[target * R_DEV + j]
            parts.append(
                request_partial(
                    queries[:, j * SLOT : (j + 1) * SLOT],
                    kbuf[chosen],
                    vbuf[chosen].astype(F32).T.astype(BF16),
                    False,
                )
            )
        return both_requests(*parts)

    def send_up(slot):
        return remote(upward.at[slot], upward.at[slot], psend.at[0, slot], precv.at[0, slot], req=me + 2)

    def send_down(slot):
        return remote(downward.at[slot], downward.at[slot], psend.at[1, slot], precv.at[1, slot], req=me - 2)

    def climb(slot):
        upward[slot] = pack_partial(cached(slot))

    def climb_merged(slot):
        own = cached(slot)
        send_up(slot).wait_recv()
        upward[slot] = pack_partial(merge(own, unpack_partial(upward[slot])))

    def descend(slot):
        downward[slot] = pack_partial(cached(slot))

    def descend_merged(slot):
        own = cached(slot)
        send_down(slot).wait_recv()
        downward[slot] = pack_partial(merge(own, unpack_partial(downward[slot])))

    def return_step(step, carry):
        high = (nz - 1 - step // 2) * 2 + step % 2
        low = step

        @pl.when(high // 2 > z)
        def _():
            pl.when(not_first)(lambda: climb_merged(high))
            pl.when(z == 0)(lambda: climb(high))
            send_up(high).start()

        @pl.when(low // 2 < z)
        def _():
            pl.when(not_last)(lambda: descend_merged(low))
            pl.when(z == nz - 1)(lambda: descend(low))
            send_down(low).start()

        return carry

    lax.fori_loop(0, (nz - 1) * 2, return_step, 0)

    own = both_requests(
        *[
            request_partial(
                qbuf[me, :, pl.ds(j * SLOT, SLOT)],
                own_k[pl.ds(j * SLOT, SLOT), :],
                own_v[:, pl.ds(j * SLOT, SLOT)],
                True,
            )
            for j in range(R_DEV)
        ]
    )
    mine = merge(own, cached(me))

    cross[0] = pack_partial(cached(mate))

    @pl.when(not_first)
    def _():
        send_up(mate).wait_recv()
        cross[0] = pack_partial(merge(unpack_partial(cross[0]), unpack_partial(upward[mate])))

    @pl.when(not_last)
    def _():
        send_down(mate).wait_recv()
        cross[0] = pack_partial(merge(unpack_partial(cross[0]), unpack_partial(downward[mate])))

    to_mate = remote(cross.at[0], cross.at[1], xsend, xrecv, req=mate)
    to_mate.start()

    remote(wo_all.at[y_mate], wo_all.at[y_mate], tsend.at[0], trecv.at[0], tp=y_mate).wait_recv()
    wo_far = remote(wo_all.at[y_mate], wo_all.at[y_mate], tsend.at[2], trecv.at[2], tp=core_mate)
    wo_far.start()

    nothing = [(jnp.zeros((HDIM, ROWS), F32), jnp.full((1, ROWS), NEGATIVE, F32), jnp.zeros((1, ROWS), F32))] * LOCAL_HEADS

    @pl.when(z == 0)
    def _():
        upward[me] = jnp.zeros(upward.shape[1:], BF16)

    @pl.when(not_first)
    def _():
        send_up(me).wait_recv()

    @pl.when(z == nz - 1)
    def _():
        downward[me] = jnp.zeros(downward.shape[1:], BF16)

    @pl.when(not_last)
    def _():
        send_down(me).wait_recv()

    def present(condition, partial):
        return [
            (numer, jnp.where(condition, top, empty), total)
            for (numer, top, total), (_, empty, _) in zip(partial, nothing)
        ]

    mine = merge(mine, present(not_first, unpack_partial(upward[me])))
    mine = merge(mine, present(not_last, unpack_partial(downward[me])))
    to_mate.wait_recv()
    mine = merge(mine, unpack_partial(cross[1]))
    att[tp] = jnp.concatenate([(numer / total).astype(BF16) for numer, _, total in mine], axis=0)

    att_y = remote(att.at[tp], att.at[tp], tsend.at[3], trecv.at[3], tp=y_mate)
    att_core = remote(att.at[tp], att.at[tp], tsend.at[4], trecv.at[4], tp=core_mate)
    att_y.start()
    att_core.start()

    def projected(index):
        return matmul(att[index].astype(F32).T.astype(BF16), wo_all[index])

    terms = projected(tp)
    remote(wo_all.at[core_mate], wo_all.at[core_mate], tsend.at[1], trecv.at[1], tp=core_mate).wait_recv()
    remote(att.at[core_mate], att.at[core_mate], tsend.at[4], trecv.at[4], tp=core_mate).wait_recv()
    terms = terms + projected(core_mate)
    remote(att.at[y_mate], att.at[y_mate], tsend.at[3], trecv.at[3], tp=y_mate).wait_recv()
    att_far = remote(att.at[y_mate], att.at[y_mate], tsend.at[5], trecv.at[5], tp=core_mate)
    att_far.start()
    terms = terms + projected(y_mate)
    diagonal = (core_mate + 2) % 4
    remote(wo_all.at[diagonal], wo_all.at[diagonal], tsend.at[2], trecv.at[2], tp=core_mate).wait_recv()
    remote(att.at[diagonal], att.at[diagonal], tsend.at[5], trecv.at[5], tp=core_mate).wait_recv()
    terms = terms + projected(diagonal)

    middle = (tokens[...].astype(F32) + terms).astype(BF16).astype(F32)
    normed_middle = normalize(middle, gain_f[...].astype(F32))
    loads[4].wait()
    gate = matmul(normed_middle, up_v[...])
    hidden_t = (gate / (1.0 + jnp.exp(-gate))).T.astype(BF16)

    def down_part(index):
        return matmul(down_t[pl.ds(pl.multiple_of(index * WIDTH, 16), WIDTH)], hidden_t)

    core_out[0] = down_part(diagonal).astype(BF16)
    core_out[1] = down_part(core_mate).astype(BF16)
    fold = remote(core_out, core_in, tsend.at[6], trecv.at[6], tp=core_mate)
    fold.start()
    far_part = down_part(y_mate)
    near_part = down_part(tp)
    mid_t[...] = middle.T
    near_part = near_part + mid_t[pl.ds(pl.multiple_of(tp * WIDTH, 16), WIDTH)]
    fold.wait_recv()
    y_out[...] = (far_part + core_in[0].astype(F32)).astype(BF16)
    swap = remote(y_out, y_in, tsend.at[7], trecv.at[7], tp=y_mate)
    swap.start()
    near_part = near_part + core_in[1].astype(F32)
    lane = lax.broadcasted_iota(jnp.int32, (WIDTH, ROWS), 1)
    live = jnp.where(lane < SLOT, length[me * R_DEV], length[me * R_DEV + 1])
    swap.wait_recv()
    layer = near_part + y_in[...].astype(F32)
    out[...] = jnp.where(lane % SLOT < live, layer, 0.0).T.astype(BF16)

    over_whole.wait_send()

    def sent_step(plane, carry):
        pl.when(plane != z)(lambda: over_late(plane).wait_send())

        @pl.when(jnp.logical_and(not_last, plane <= z))
        def _():
            up_whole(plane).wait_send()
            up_early(plane).wait_send()

        @pl.when(jnp.logical_and(not_first, plane >= z))
        def _():
            down_whole(plane).wait_send()
            down_early(plane).wait_send()

        for column in range(2):
            slot = plane * 2 + column
            pl.when(plane > z)(lambda: send_up(slot).wait_send())
            pl.when(plane < z)(lambda: send_down(slot).wait_send())
        return carry

    lax.fori_loop(0, nz, sent_step, 0)
    for copy in (to_mate, wo_y, wo_core, wo_far, att_y, att_core, att_far, fold, swap):
        copy.wait_send()


def per_device(
    tokens,
    attention_gain,
    feedforward_gain,
    query_weight,
    key_weight,
    value_weight,
    out_weight,
    up_weight,
    down_weight,
    cache_keys,
    cache_values,
    request_prefix,
    suffix_length,
):
    owners = lax.axis_size("req")
    nz = owners // 2
    rows, model = tokens.shape
    prefixes = cache_keys.shape[1]
    dma = pltpu.SemaphoreType.DMA
    vmem = pl.BlockSpec(memory_space=pltpu.VMEM)
    smem = pl.BlockSpec(memory_space=pltpu.SMEM)
    away = pl.BlockSpec(memory_space=pl.ANY)
    return pl.pallas_call(
        functools.partial(kernel, nz),
        out_shape=jax.ShapeDtypeStruct((rows, WIDTH), BF16),
        in_specs=[vmem] * 6 + [away] * 5 + [smem] * 2,
        out_specs=vmem,
        scratch_shapes=[
            pltpu.VMEM((owners, WIDTH, ROWS), BF16),
            pltpu.VMEM((prefixes, PG, WIDTH), BF16),
            pltpu.VMEM((prefixes, PG, WIDTH), BF16),
            pltpu.VMEM((4, WIDTH, model), BF16),
            pltpu.VMEM((model, WIDTH), BF16),
            pltpu.VMEM((WIDTH, model), BF16),
            pltpu.VMEM((model, WIDTH), BF16),
            pltpu.VMEM((ROWS, WIDTH), BF16),
            pltpu.VMEM((WIDTH, ROWS), BF16),
            pltpu.VMEM((owners, WIDTH + STATS, ROWS), BF16),
            pltpu.VMEM((owners, WIDTH + STATS, ROWS), BF16),
            pltpu.VMEM((2, WIDTH + STATS, ROWS), BF16),
            pltpu.VMEM((4, WIDTH, ROWS), BF16),
            pltpu.VMEM((2, WIDTH, ROWS), BF16),
            pltpu.VMEM((2, WIDTH, ROWS), BF16),
            pltpu.VMEM((WIDTH, ROWS), BF16),
            pltpu.VMEM((WIDTH, ROWS), BF16),
            pltpu.VMEM((model, ROWS), F32),
            dma((5,)),
            dma((5, nz)),
            dma((3, nz)),
            dma((2, owners)),
            dma((2, owners)),
            dma,
            dma,
            dma((8,)),
            dma((8,)),
        ],
        compiler_params=pltpu.CompilerParams(
            collective_id=0, has_side_effects=True, vmem_limit_bytes=60 * 1024 * 1024
        ),
    )(
        tokens,
        attention_gain.reshape(1, model),
        feedforward_gain.reshape(1, model),
        query_weight,
        key_weight,
        value_weight,
        out_weight,
        up_weight,
        down_weight,
        cache_keys[0],
        cache_values[0],
        request_prefix,
        suffix_length,
    )


def solution(mesh):
    in_specs = (
        P("req", None),
        P(),
        P(),
        P(None, "tp"),
        P(None, "tp"),
        P(None, "tp"),
        P("tp", None),
        P(None, "tp"),
        P("tp", None),
        P("req", None, None, "tp"),
        P("req", None, None, "tp"),
        P(),
        P(),
    )
    out_specs = P("req", "tp")
    return jax.shard_map(
        per_device, mesh=mesh, in_specs=in_specs, out_specs=out_specs, check_vma=False
    )
```

```python
import functools
import math

import jax
import jax.numpy as jnp
from jax import lax
from jax.experimental import pallas as pl
from jax.experimental.pallas import tpu as pltpu
from jax.sharding import PartitionSpec as P

HDIM = 80
SLOT = 128
R_DEV = 2
PG = 192
LOCAL_HEADS = 4
WIDTH = HDIM * LOCAL_HEADS
ROWS = R_DEV * SLOT
STATS = 16
HALF = WIDTH // 2

EPSILON = 1e-06
NEGATIVE = -1e30
MESH = pl.DeviceIdType.MESH
F32 = jnp.float32
BF16 = jnp.bfloat16


def normalize(floats, gain):
    mean_square = jnp.mean(floats * floats, axis=-1, keepdims=True)
    return (floats * lax.rsqrt(mean_square + EPSILON) * gain).astype(BF16)


def matmul(left, right):
    return jnp.dot(left, right, preferred_element_type=F32)


def matmul_rows(left, right):
    return lax.dot_general(left, right, (((1,), (1,)), ((), ())), preferred_element_type=F32)


def head_rows(values, head):
    return values[head * HDIM : (head + 1) * HDIM]


def request_partial(query_t, keys, values_t, causal):
    none = jnp.zeros((HDIM, SLOT), BF16)
    spread = jnp.concatenate(
        [
            jnp.concatenate(
                [head_rows(query_t, h) if g == h else none for g in range(LOCAL_HEADS)], axis=1
            )
            for h in range(LOCAL_HEADS)
        ],
        axis=0,
    )
    scores = matmul(keys, spread) * (1.0 / math.sqrt(HDIM))
    if causal:
        key_row = lax.broadcasted_iota(jnp.int32, scores.shape, 0)
        query_row = lax.broadcasted_iota(jnp.int32, scores.shape, 1) % SLOT
        scores = jnp.where(key_row <= query_row, scores, NEGATIVE)
    top = jnp.max(scores, axis=0, keepdims=True)
    if not causal:
        top = top.astype(BF16).astype(F32)
    weights = jnp.exp(scores - top)
    total = jnp.sum(weights, axis=0, keepdims=True)
    numer = matmul(values_t, weights.astype(BF16))
    lanes = [slice(h * SLOT, (h + 1) * SLOT) for h in range(LOCAL_HEADS)]
    return [(head_rows(numer, h)[:, lanes[h]], top[:, lanes[h]], total[:, lanes[h]]) for h in range(LOCAL_HEADS)]


def both_requests(first, second):
    return [
        tuple(jnp.concatenate([a, b], axis=1) for a, b in zip(first[h], second[h]))
        for h in range(LOCAL_HEADS)
    ]


def merge(one, other):
    merged = []
    for (numer_a, top_a, total_a), (numer_b, top_b, total_b) in zip(one, other):
        top = jnp.maximum(top_a, top_b)
        factor_a = jnp.exp(top_a - top)
        factor_b = jnp.exp(top_b - top)
        merged.append(
            (
                numer_a * factor_a + numer_b * factor_b,
                top,
                total_a * factor_a + total_b * factor_b,
            )
        )
    return merged


def pack_partial(partial):
    heads = len(partial)
    shares = [(numer / total).astype(BF16) for numer, _, total in partial]
    tops = [top for _, top, _ in partial]
    whole = [total.astype(BF16).astype(F32) for _, _, total in partial]
    rest = [total - high for (_, _, total), high in zip(partial, whole)]
    pad = [jnp.zeros((STATS - 3 * heads, ROWS), F32)]
    stats = jnp.concatenate(tops + whole + rest + pad, axis=0).astype(BF16)
    return jnp.concatenate(shares + [stats], axis=0)


def unpack_partial(block):
    heads = (block.shape[0] - STATS) // HDIM
    stats = block[heads * HDIM :].astype(F32)
    partial = []
    for h in range(heads):
        top = stats[h : h + 1]
        total = stats[heads + h : heads + h + 1]
        total = total + stats[2 * heads + h : 2 * heads + h + 1]
        partial.append((head_rows(block, h).astype(F32) * total, top, total))
    return partial


def kernel(
    nz,
    tokens,
    gain_a,
    gain_f,
    wq,
    wk,
    wv,
    wo,
    wup,
    wdown,
    cache_k,
    cache_v,
    prefix,
    length,
    out,
    qbuf,
    kbuf,
    vbuf,
    wo_all,
    up_v,
    down_v,
    down_t,
    own_k,
    own_v,
    cache_vt,
    numers,
    stats,
    full_way,
    half_way,
    over,
    cross,
    att,
    core_out,
    core_in,
    y_out,
    y_in,
    mid_t,
    local_sem,
    qsend,
    qrecv,
    psend,
    precv,
    xsend,
    xrecv,
    tsend,
    trecv,
    osend,
    orecv,
):
    me = lax.axis_index("req")
    tp = lax.axis_index("tp")
    z = me // 2
    x = me % 2
    mate = z * 2 + 1 - x
    core_mate = tp + 1 - 2 * (tp % 2)
    y_mate = (tp + 2) % 4
    not_first = z > 0
    not_last = z < nz - 1

    def remote(source, target, send_sem, recv_sem, **where):
        return pltpu.make_async_remote_copy(
            src_ref=source,
            dst_ref=target,
            send_sem=send_sem,
            recv_sem=recv_sem,
            device_id=where,
            device_id_type=MESH,
        )

    barrier = pltpu.get_barrier_semaphore()

    def greet(**where):
        pl.semaphore_signal(barrier, inc=1, device_id=where, device_id_type=MESH)

    greet(req=mate)
    greet(tp=core_mate)
    greet(tp=y_mate)
    pl.when(not_first)(lambda: greet(req=me - 2))
    pl.when(not_last)(lambda: greet(req=me + 2))

    loads = [
        pltpu.make_async_copy(source, target, local_sem.at[i])
        for i, (source, target) in enumerate(
            [(wo, wo_all.at[tp]), (cache_k, kbuf), (cache_v, vbuf), (wdown, down_v), (wup, up_v)]
        )
    ]
    for load in loads:
        load.start()

    normed = normalize(tokens[...].astype(F32), gain_a[...].astype(F32)[None, :])
    qbuf[me] = matmul_rows(wq[...], normed).astype(BF16)

    pl.semaphore_wait(barrier, 3 + jnp.where(not_first, 1, 0) + jnp.where(not_last, 1, 0))

    def whole(plane, column):
        return qbuf.at[plane * 2 + column]

    def early(plane, column):
        return qbuf.at[plane * 2 + column, pl.ds(0, HALF)]

    def late(plane, column):
        return qbuf.at[plane * 2 + column, pl.ds(HALF, HALF)]

    def up_whole(plane):
        return remote(whole(plane, x), whole(plane, x), qsend.at[0, plane], qrecv.at[0, plane], req=me + 2)

    def up_early(plane):
        return remote(early(plane, 1 - x), early(plane, 1 - x), qsend.at[1, plane], qrecv.at[1, plane], req=me + 2)

    def down_whole(plane):
        return remote(whole(plane, x), whole(plane, x), qsend.at[2, plane], qrecv.at[0, plane], req=me - 2)

    def down_early(plane):
        return remote(early(plane, 1 - x), early(plane, 1 - x), qsend.at[3, plane], qrecv.at[1, plane], req=me - 2)

    def over_late(plane):
        return remote(late(plane, x), late(plane, x), qsend.at[4, plane], qrecv.at[2, plane], req=mate)

    over_whole = remote(whole(z, x), whole(z, x), qsend.at[4, z], qrecv.at[2, z], req=mate)
    got_whole = remote(whole(z, 1 - x), whole(z, 1 - x), qsend.at[4, z], qrecv.at[2, z], req=mate)

    over_whole.start()
    pl.when(not_last)(lambda: up_whole(z).start())
    pl.when(not_first)(lambda: down_whole(z).start())

    loads[0].wait()
    wo_y = remote(wo_all.at[tp], wo_all.at[tp], tsend.at[0], trecv.at[0], tp=y_mate)
    wo_core = remote(wo_all.at[tp], wo_all.at[tp], tsend.at[1], trecv.at[1], tp=core_mate)
    wo_y.start()
    wo_core.start()

    got_whole.wait_recv()
    pl.when(not_last)(lambda: up_early(z).start())
    pl.when(not_first)(lambda: down_early(z).start())

    own_k[...] = matmul_rows(normed, wk[...]).astype(BF16)
    own_v[...] = matmul_rows(wv[...], normed).astype(BF16)

    def save(way, column, partial):
        for h, (numer, top, total) in enumerate(partial):
            numers[way, column, pl.ds(h * HDIM, HDIM)] = numer
            stats[way, column, pl.ds(h, 1)] = top
            stats[way, column, pl.ds(LOCAL_HEADS + h, 1)] = total

    def load(way, column):
        held = stats[way, column]
        return [
            (
                numers[way, column, pl.ds(h * HDIM, HDIM)],
                held[h : h + 1],
                held[LOCAL_HEADS + h : LOCAL_HEADS + h + 1],
            )
            for h in range(LOCAL_HEADS)
        ]

    def cached(target):
        queries = qbuf[target]
        parts = []
        for j in range(R_DEV):
            chosen = prefix[target * R_DEV + j]
            parts.append(
                request_partial(
                    queries[:, j * SLOT : (j + 1) * SLOT], kbuf[chosen], cache_vt[chosen], False
                )
            )
        return both_requests(*parts)

    save(
        2,
        1,
        both_requests(
            *[
                request_partial(
                    qbuf[me, :, pl.ds(j * SLOT, SLOT)],
                    own_k[pl.ds(j * SLOT, SLOT), :],
                    own_v[:, pl.ds(j * SLOT, SLOT)],
                    True,
                )
                for j in range(R_DEV)
            ]
        ),
    )

    def gather_step(step, carry):
        below = z - 1 - step
        above = z + 1 + step

        @pl.when(below >= 0)
        def _():
            up_whole(below).wait_recv()
            pl.when(not_last)(lambda: up_whole(below).start())
            over_late(below).start()

        @pl.when(above < nz)
        def _():
            down_whole(above).wait_recv()
            pl.when(not_first)(lambda: down_whole(above).start())
            over_late(above).start()

        @pl.when(below >= 0)
        def _():
            up_early(below).wait_recv()
            pl.when(not_last)(lambda: up_early(below).start())

        @pl.when(above < nz)
        def _():
            down_early(above).wait_recv()
            pl.when(not_first)(lambda: down_early(above).start())

        @pl.when(step == 0)
        def _():
            loads[1].wait()
            loads[2].wait()

            def turn(index, inner):
                cache_vt[index] = vbuf[index].astype(F32).T.astype(BF16)
                return inner

            lax.fori_loop(0, vbuf.shape[0], turn, 0)

        pl.when(step == min(1, nz - 2))(lambda: save(2, 1, merge(load(2, 1), cached(me))))
        pl.when(step == min(2, nz - 2))(lambda: save(2, 0, cached(mate)))
        return carry

    lax.fori_loop(0, nz - 1, gather_step, 0)

    def late_step(plane, carry):
        @pl.when(plane != z)
        def _():
            remote(late(plane, 1 - x), late(plane, 1 - x), qsend.at[4, plane], qrecv.at[2, plane], req=mate).wait_recv()

        return carry

    lax.fori_loop(0, nz, late_step, 0)
    def send_over(plane):
        return remote(over.at[0, plane], over.at[1, plane], osend.at[plane], orecv.at[plane], req=mate)

    def send_half(way, plane):
        there = me + 2 - 4 * way
        return remote(
            half_way.at[way, plane], half_way.at[way, plane], psend.at[0, way, plane], precv.at[0, way, plane], req=there
        )

    def send_full(way, plane):
        there = me + 2 - 4 * way
        return remote(
            full_way.at[way, plane], full_way.at[way, plane], psend.at[1, way, plane], precv.at[1, way, plane], req=there
        )

    def compute(way, plane):
        far = cached(plane * 2 + 1 - x)
        save(way, 0, far)
        over[0, plane] = pack_partial(far[2:])
        send_over(plane).start()
        save(way, 1, cached(plane * 2 + x))

    def finish(way, plane, has_source):
        @pl.when(has_source)
        def _():
            send_half(way, plane).wait_recv()
            half_way[way, plane] = pack_partial(merge(load(way, 0)[:2], unpack_partial(half_way[way, plane])))

        @pl.when(jnp.logical_not(has_source))
        def _():
            half_way[way, plane] = pack_partial(load(way, 0)[:2])

        send_half(way, plane).start()
        send_over(plane).wait_recv()
        near = load(way, 1)
        near = near[:2] + merge(near[2:], unpack_partial(over[1, plane]))

        @pl.when(has_source)
        def _():
            send_full(way, plane).wait_recv()
            full_way[way, plane] = pack_partial(merge(near, unpack_partial(full_way[way, plane])))

        @pl.when(jnp.logical_not(has_source))
        def _():
            full_way[way, plane] = pack_partial(near)

        send_full(way, plane).start()

    def return_step(step, carry):
        high = nz - 1 - step
        low = step
        pl.when(high > z)(lambda: compute(0, high))
        pl.when(low < z)(lambda: compute(1, low))
        pl.when(high > z)(lambda: finish(0, high, not_first))
        pl.when(low < z)(lambda: finish(1, low, not_last))
        return carry

    over[0, z] = pack_partial(load(2, 0)[2:])
    send_over(z).start()
    lax.fori_loop(0, nz - 1, return_step, 0)

    def gather_in(way, condition, send, place, held):
        @pl.when(condition)
        def _():
            send(way, z).wait_recv()

        @pl.when(jnp.logical_not(condition))
        def _():
            place[way, z] = jnp.zeros(place.shape[2:], BF16)

        arrived = unpack_partial(place[way, z])
        arrived = [(numer, jnp.where(condition, top, NEGATIVE), total) for numer, top, total in arrived]
        return merge(held, arrived)

    half = load(2, 0)[:2]
    half = gather_in(0, not_first, send_half, half_way, half)
    half = gather_in(1, not_last, send_half, half_way, half)
    cross[0] = pack_partial(half)
    to_mate = remote(cross.at[0], cross.at[1], xsend, xrecv, req=mate)
    to_mate.start()

    remote(wo_all.at[y_mate], wo_all.at[y_mate], tsend.at[0], trecv.at[0], tp=y_mate).wait_recv()
    wo_far = remote(wo_all.at[y_mate], wo_all.at[y_mate], tsend.at[2], trecv.at[2], tp=core_mate)
    wo_far.start()

    loads[3].wait()
    down_t[...] = down_v[...].astype(F32).T.astype(BF16)
    send_over(z).wait_recv()
    mine = load(2, 1)
    mine = mine[:2] + merge(mine[2:], unpack_partial(over[1, z]))
    mine = gather_in(0, not_first, send_full, full_way, mine)
    mine = gather_in(1, not_last, send_full, full_way, mine)
    to_mate.wait_recv()
    mine = merge(mine[:2], unpack_partial(cross[1])) + mine[2:]
    att[tp] = jnp.concatenate([(numer / total).astype(BF16) for numer, _, total in mine], axis=0)

    att_y = remote(att.at[tp], att.at[tp], tsend.at[3], trecv.at[3], tp=y_mate)
    att_core = remote(att.at[tp], att.at[tp], tsend.at[4], trecv.at[4], tp=core_mate)
    att_y.start()
    att_core.start()

    def projected(index):
        return matmul(att[index].astype(F32).T.astype(BF16), wo_all[index])

    terms = projected(tp)
    remote(wo_all.at[core_mate], wo_all.at[core_mate], tsend.at[1], trecv.at[1], tp=core_mate).wait_recv()
    remote(att.at[core_mate], att.at[core_mate], tsend.at[4], trecv.at[4], tp=core_mate).wait_recv()
    terms = terms + projected(core_mate)
    remote(att.at[y_mate], att.at[y_mate], tsend.at[3], trecv.at[3], tp=y_mate).wait_recv()
    att_far = remote(att.at[y_mate], att.at[y_mate], tsend.at[5], trecv.at[5], tp=core_mate)
    att_far.start()
    terms = terms + projected(y_mate)
    diagonal = (core_mate + 2) % 4
    remote(wo_all.at[diagonal], wo_all.at[diagonal], tsend.at[2], trecv.at[2], tp=core_mate).wait_recv()
    remote(att.at[diagonal], att.at[diagonal], tsend.at[5], trecv.at[5], tp=core_mate).wait_recv()
    terms = terms + projected(diagonal)

    middle = (tokens[...].astype(F32) + terms).astype(BF16).astype(F32)
    normed_middle = normalize(middle, gain_f[...].astype(F32)[None, :])
    loads[4].wait()
    gate = matmul_rows(up_v[...], normed_middle)
    hidden_t = (gate / (1.0 + jnp.exp(-gate))).astype(BF16)

    def down_part(index):
        return matmul(down_t[pl.ds(pl.multiple_of(index * WIDTH, 16), WIDTH)], hidden_t)

    core_out[0] = down_part(diagonal).astype(BF16)
    core_out[1] = down_part(core_mate).astype(BF16)
    fold = remote(core_out, core_in, tsend.at[6], trecv.at[6], tp=core_mate)
    fold.start()
    far_part = down_part(y_mate)
    near_part = down_part(tp)
    mid_t[...] = middle.T
    near_part = near_part + mid_t[pl.ds(pl.multiple_of(tp * WIDTH, 16), WIDTH)]
    fold.wait_recv()
    y_out[...] = (far_part + core_in[0].astype(F32)).astype(BF16)
    swap = remote(y_out, y_in, tsend.at[7], trecv.at[7], tp=y_mate)
    swap.start()
    near_part = near_part + core_in[1].astype(F32)
    lane = lax.broadcasted_iota(jnp.int32, (WIDTH, ROWS), 1)
    live = jnp.where(lane < SLOT, length[me * R_DEV], length[me * R_DEV + 1])
    swap.wait_recv()
    layer = near_part + y_in[...].astype(F32)
    out[...] = jnp.where(lane % SLOT < live, layer, 0.0).astype(BF16)

    over_whole.wait_send()

    def sent_step(plane, carry):
        pl.when(plane != z)(lambda: over_late(plane).wait_send())

        @pl.when(jnp.logical_and(not_last, plane <= z))
        def _():
            up_whole(plane).wait_send()
            up_early(plane).wait_send()

        @pl.when(jnp.logical_and(not_first, plane >= z))
        def _():
            down_whole(plane).wait_send()
            down_early(plane).wait_send()

        send_over(plane).wait_send()

        @pl.when(plane > z)
        def _():
            send_half(0, plane).wait_send()
            send_full(0, plane).wait_send()

        @pl.when(plane < z)
        def _():
            send_half(1, plane).wait_send()
            send_full(1, plane).wait_send()

        return carry

    lax.fori_loop(0, nz, sent_step, 0)
    for copy in (to_mate, wo_y, wo_core, wo_far, att_y, att_core, att_far, fold, swap):
        copy.wait_send()


def per_device(
    tokens,
    attention_gain,
    feedforward_gain,
    query_weight,
    key_weight,
    value_weight,
    out_weight,
    up_weight,
    down_weight,
    cache_keys,
    cache_values,
    request_prefix,
    suffix_length,
):
    owners = lax.axis_size("req")
    nz = owners // 2
    rows, model = tokens.shape
    prefixes = cache_keys.shape[1]
    dma = pltpu.SemaphoreType.DMA
    vmem = pl.BlockSpec(memory_space=pltpu.VMEM)
    smem = pl.BlockSpec(memory_space=pltpu.SMEM)
    away = pl.BlockSpec(memory_space=pl.ANY)
    return pl.pallas_call(
        functools.partial(kernel, nz),
        out_shape=jax.ShapeDtypeStruct((WIDTH, rows), BF16),
        in_specs=[vmem] * 6 + [away] * 5 + [smem] * 2,
        out_specs=vmem,
        scratch_shapes=[
            pltpu.VMEM((owners, WIDTH, ROWS), BF16),
            pltpu.VMEM((prefixes, PG, WIDTH), BF16),
            pltpu.VMEM((prefixes, PG, WIDTH), BF16),
            pltpu.VMEM((4, WIDTH, model), BF16),
            pltpu.VMEM((WIDTH, model), BF16),
            pltpu.VMEM((WIDTH, model), BF16),
            pltpu.VMEM((model, WIDTH), BF16),
            pltpu.VMEM((ROWS, WIDTH), BF16),
            pltpu.VMEM((WIDTH, ROWS), BF16),
            pltpu.VMEM((prefixes, WIDTH, PG), BF16),
            pltpu.VMEM((3, 2, WIDTH, ROWS), F32),
            pltpu.VMEM((3, 2, 2 * LOCAL_HEADS, ROWS), F32),
            pltpu.VMEM((2, nz, WIDTH + STATS, ROWS), BF16),
            pltpu.VMEM((2, nz, HALF + STATS, ROWS), BF16),
            pltpu.VMEM((2, nz, HALF + STATS, ROWS), BF16),
            pltpu.VMEM((2, HALF + STATS, ROWS), BF16),
            pltpu.VMEM((4, WIDTH, ROWS), BF16),
            pltpu.VMEM((2, WIDTH, ROWS), BF16),
            pltpu.VMEM((2, WIDTH, ROWS), BF16),
            pltpu.VMEM((WIDTH, ROWS), BF16),
            pltpu.VMEM((WIDTH, ROWS), BF16),
            pltpu.VMEM((model, ROWS), F32),
            dma((5,)),
            dma((5, nz)),
            dma((3, nz)),
            dma((2, 2, nz)),
            dma((2, 2, nz)),
            dma,
            dma,
            dma((8,)),
            dma((8,)),
            dma((nz,)),
            dma((nz,)),
        ],
        compiler_params=pltpu.CompilerParams(
            collective_id=0, has_side_effects=True, vmem_limit_bytes=60 * 1024 * 1024
        ),
    )(
        tokens,
        attention_gain,
        feedforward_gain,
        query_weight.T,
        key_weight.T,
        value_weight.T,
        out_weight,
        up_weight.T,
        down_weight,
        cache_keys[0],
        cache_values[0],
        request_prefix,
        suffix_length,
    ).T


def solution(mesh):
    in_specs = (
        P("req", None),
        P(),
        P(),
        P(None, "tp"),
        P(None, "tp"),
        P(None, "tp"),
        P("tp", None),
        P(None, "tp"),
        P("tp", None),
        P("req", None, None, "tp"),
        P("req", None, None, "tp"),
        P(),
        P(),
    )
    out_specs = P("req", "tp")
    return jax.shard_map(
        per_device, mesh=mesh, in_specs=in_specs, out_specs=out_specs, check_vma=False
    )
```

```python
import functools
import math

import jax
import jax.numpy as jnp
from jax import lax
from jax.experimental import pallas as pl
from jax.experimental.pallas import tpu as pltpu
from jax.sharding import PartitionSpec as P

HDIM = 80
SLOT = 128
R_DEV = 2
PG = 192
LOCAL_HEADS = 4
WIDTH = HDIM * LOCAL_HEADS
ROWS = R_DEV * SLOT
STATS = 16
FIRST = HDIM
REST = WIDTH - HDIM

EPSILON = 1e-06
NEGATIVE = -1e30
MESH = pl.DeviceIdType.MESH
F32 = jnp.float32
BF16 = jnp.bfloat16


def normalize(floats, gain):
    mean_square = jnp.mean(floats * floats, axis=-1, keepdims=True)
    return (floats * lax.rsqrt(mean_square + EPSILON) * gain).astype(BF16)


def matmul(left, right):
    return jnp.dot(left, right, preferred_element_type=F32)


def matmul_rows(left, right):
    return lax.dot_general(left, right, (((1,), (1,)), ((), ())), preferred_element_type=F32)


def head_rows(values, head):
    return values[head * HDIM : (head + 1) * HDIM]


def request_partial(query_t, keys, values_t, causal):
    none = jnp.zeros((HDIM, SLOT), BF16)
    spread = jnp.concatenate(
        [
            jnp.concatenate(
                [head_rows(query_t, h) if g == h else none for g in range(LOCAL_HEADS)], axis=1
            )
            for h in range(LOCAL_HEADS)
        ],
        axis=0,
    )
    scores = matmul(keys, spread) * (1.0 / math.sqrt(HDIM))
    if causal:
        key_row = lax.broadcasted_iota(jnp.int32, scores.shape, 0)
        query_row = lax.broadcasted_iota(jnp.int32, scores.shape, 1) % SLOT
        scores = jnp.where(key_row <= query_row, scores, NEGATIVE)
    top = jnp.max(scores, axis=0, keepdims=True)
    if not causal:
        top = top.astype(BF16).astype(F32)
    weights = jnp.exp(scores - top)
    total = jnp.sum(weights, axis=0, keepdims=True)
    numer = matmul(values_t, weights.astype(BF16))
    lanes = [slice(h * SLOT, (h + 1) * SLOT) for h in range(LOCAL_HEADS)]
    return [(head_rows(numer, h)[:, lanes[h]], top[:, lanes[h]], total[:, lanes[h]]) for h in range(LOCAL_HEADS)]


def both_requests(first, second):
    return [
        tuple(jnp.concatenate([a, b], axis=1) for a, b in zip(first[h], second[h]))
        for h in range(LOCAL_HEADS)
    ]


def merge(one, other):
    merged = []
    for (numer_a, top_a, total_a), (numer_b, top_b, total_b) in zip(one, other):
        top = jnp.maximum(top_a, top_b)
        factor_a = jnp.exp(top_a - top)
        factor_b = jnp.exp(top_b - top)
        merged.append(
            (
                numer_a * factor_a + numer_b * factor_b,
                top,
                total_a * factor_a + total_b * factor_b,
            )
        )
    return merged


def pack_partial(partial):
    heads = len(partial)
    shares = [(numer / total).astype(BF16) for numer, _, total in partial]
    tops = [top for _, top, _ in partial]
    whole = [total.astype(BF16).astype(F32) for _, _, total in partial]
    rest = [total - high for (_, _, total), high in zip(partial, whole)]
    pad = [jnp.zeros((STATS - 3 * heads, ROWS), F32)]
    stats = jnp.concatenate(tops + whole + rest + pad, axis=0).astype(BF16)
    return jnp.concatenate(shares + [stats], axis=0)


def unpack_partial(block):
    heads = (block.shape[0] - STATS) // HDIM
    stats = block[heads * HDIM :].astype(F32)
    partial = []
    for h in range(heads):
        top = stats[h : h + 1]
        total = stats[heads + h : heads + h + 1]
        total = total + stats[2 * heads + h : 2 * heads + h + 1]
        partial.append((head_rows(block, h).astype(F32) * total, top, total))
    return partial


def kernel(
    nz,
    tokens,
    gain_a,
    gain_f,
    wq,
    wk,
    wv,
    wo,
    wup,
    wdown,
    cache_k,
    cache_v,
    prefix,
    length,
    out,
    qbuf,
    kbuf,
    vbuf,
    wo_all,
    up_v,
    down_v,
    down_t,
    own_k,
    own_v,
    cache_vt,
    numers,
    stats,
    rest_way,
    first_way,
    over,
    cross,
    att,
    core_out,
    core_in,
    y_out,
    y_in,
    mid_t,
    local_sem,
    qsend,
    qrecv,
    psend,
    precv,
    xsend,
    xrecv,
    tsend,
    trecv,
    osend,
    orecv,
):
    me = lax.axis_index("req")
    tp = lax.axis_index("tp")
    z = me // 2
    x = me % 2
    mate = z * 2 + 1 - x
    core_mate = tp + 1 - 2 * (tp % 2)
    y_mate = (tp + 2) % 4
    not_first = z > 0
    not_last = z < nz - 1

    def remote(source, target, send_sem, recv_sem, **where):
        return pltpu.make_async_remote_copy(
            src_ref=source,
            dst_ref=target,
            send_sem=send_sem,
            recv_sem=recv_sem,
            device_id=where,
            device_id_type=MESH,
        )

    barrier = pltpu.get_barrier_semaphore()

    def greet(**where):
        pl.semaphore_signal(barrier, inc=1, device_id=where, device_id_type=MESH)

    greet(req=mate)
    greet(tp=core_mate)
    greet(tp=y_mate)
    pl.when(not_first)(lambda: greet(req=me - 2))
    pl.when(not_last)(lambda: greet(req=me + 2))

    loads = [
        pltpu.make_async_copy(source, target, local_sem.at[i])
        for i, (source, target) in enumerate(
            [(wo, wo_all.at[tp]), (cache_k, kbuf), (cache_v, vbuf), (wdown, down_v), (wup, up_v)]
        )
    ]
    for load in loads:
        load.start()

    normed = normalize(tokens[...].astype(F32), gain_a[...].astype(F32)[None, :])
    qbuf[me] = matmul_rows(wq[...], normed).astype(BF16)

    pl.semaphore_wait(barrier, 3 + jnp.where(not_first, 1, 0) + jnp.where(not_last, 1, 0))

    def whole(plane, column):
        return qbuf.at[plane * 2 + column]

    def early(plane, column):
        return qbuf.at[plane * 2 + column, pl.ds(0, FIRST)]

    def late(plane, column):
        return qbuf.at[plane * 2 + column, pl.ds(FIRST, REST)]

    def up_whole(plane):
        return remote(whole(plane, x), whole(plane, x), qsend.at[0, plane], qrecv.at[0, plane], req=me + 2)

    def up_early(plane):
        return remote(early(plane, 1 - x), early(plane, 1 - x), qsend.at[1, plane], qrecv.at[1, plane], req=me + 2)

    def down_whole(plane):
        return remote(whole(plane, x), whole(plane, x), qsend.at[2, plane], qrecv.at[0, plane], req=me - 2)

    def down_early(plane):
        return remote(early(plane, 1 - x), early(plane, 1 - x), qsend.at[3, plane], qrecv.at[1, plane], req=me - 2)

    def over_late(plane):
        return remote(late(plane, x), late(plane, x), qsend.at[4, plane], qrecv.at[2, plane], req=mate)

    over_whole = remote(whole(z, x), whole(z, x), qsend.at[4, z], qrecv.at[2, z], req=mate)
    got_whole = remote(whole(z, 1 - x), whole(z, 1 - x), qsend.at[4, z], qrecv.at[2, z], req=mate)

    over_whole.start()
    pl.when(not_last)(lambda: up_whole(z).start())
    pl.when(not_first)(lambda: down_whole(z).start())

    loads[0].wait()
    wo_y = remote(wo_all.at[tp], wo_all.at[tp], tsend.at[0], trecv.at[0], tp=y_mate)
    wo_core = remote(wo_all.at[tp], wo_all.at[tp], tsend.at[1], trecv.at[1], tp=core_mate)
    wo_y.start()
    wo_core.start()

    got_whole.wait_recv()
    pl.when(not_last)(lambda: up_early(z).start())
    pl.when(not_first)(lambda: down_early(z).start())

    own_k[...] = matmul_rows(normed, wk[...]).astype(BF16)
    own_v[...] = matmul_rows(wv[...], normed).astype(BF16)

    def save(plane, start, partial):
        for place, (numer, top, total) in enumerate(partial, start):
            numers[plane, pl.ds(place * HDIM, HDIM)] = numer
            stats[plane, pl.ds(place, 1)] = top
            stats[plane, pl.ds(8 + place, 1)] = total

    def load(plane, start, stop):
        held = stats[plane]
        return [
            (
                numers[plane, pl.ds(place * HDIM, HDIM)],
                held[place : place + 1],
                held[8 + place : 9 + place],
            )
            for place in range(start, stop)
        ]

    def cached(target):
        queries = qbuf[target]
        parts = []
        for j in range(R_DEV):
            chosen = prefix[target * R_DEV + j]
            parts.append(
                request_partial(
                    queries[:, j * SLOT : (j + 1) * SLOT], kbuf[chosen], cache_vt[chosen], False
                )
            )
        return both_requests(*parts)

    save(
        z,
        1,
        both_requests(
            *[
                request_partial(
                    qbuf[me, :, pl.ds(j * SLOT, SLOT)],
                    own_k[pl.ds(j * SLOT, SLOT), :],
                    own_v[:, pl.ds(j * SLOT, SLOT)],
                    True,
                )
                for j in range(R_DEV)
            ]
        ),
    )

    def relay(step):
        below = z - 1 - step
        above = z + 1 + step

        @pl.when(below >= 0)
        def _():
            up_whole(below).wait_recv()
            pl.when(not_last)(lambda: up_whole(below).start())
            over_late(below).start()

        @pl.when(above < nz)
        def _():
            down_whole(above).wait_recv()
            pl.when(not_first)(lambda: down_whole(above).start())
            over_late(above).start()

        @pl.when(below >= 0)
        def _():
            up_early(below).wait_recv()
            pl.when(not_last)(lambda: up_early(below).start())

        @pl.when(above < nz)
        def _():
            down_early(above).wait_recv()
            pl.when(not_first)(lambda: down_early(above).start())

    def turn(index, carry):
        cache_vt[index] = vbuf[index].T
        return carry

    relay(0)
    loads[1].wait()
    loads[2].wait()
    lax.fori_loop(0, vbuf.shape[0], turn, 0)

    def send_over(plane):
        return remote(over.at[0, plane], over.at[1, plane], osend.at[plane], orecv.at[plane], req=mate)

    def passing(buffer, kind, way, plane):
        there = me + 2 - 4 * way
        here_slot = jnp.where(jnp.logical_and(way == 1, plane == z), nz, plane)
        there_slot = jnp.where(jnp.logical_and(way == 1, plane == z - 1), nz, plane)
        return remote(
            buffer.at[here_slot],
            buffer.at[there_slot],
            psend.at[kind, here_slot],
            precv.at[kind, there_slot],
            req=there,
        )

    def arriving(buffer, kind, way, plane):
        slot = jnp.where(jnp.logical_and(way == 1, plane == z), nz, plane)
        copy = remote(
            buffer.at[slot], buffer.at[slot], psend.at[kind, slot], precv.at[kind, slot], req=me - 2 + 4 * way
        )
        return copy, slot

    def compute(plane):
        remote(late(plane, 1 - x), late(plane, 1 - x), qsend.at[4, plane], qrecv.at[2, plane], req=mate).wait_recv()
        far = cached(plane * 2 + 1 - x)
        save(plane, 0, far[:1])
        over[0, plane] = pack_partial(far[1:])
        send_over(plane).start()
        save(plane, 1, cached(plane * 2 + x))

    def finish(way, plane, has_source):
        def pass_on(buffer, kind, partial):
            if has_source:
                copy, slot = arriving(buffer, kind, way, plane)
                copy.wait_recv()
                partial = merge(partial, unpack_partial(buffer[slot]))
            buffer[plane] = pack_partial(partial)
            passing(buffer, kind, way, plane).start()

        pass_on(first_way, 0, load(plane, 0, 2))
        send_over(plane).wait_recv()
        pass_on(rest_way, 1, merge(load(plane, 2, 5), unpack_partial(over[1, plane])))

    def return_step(step, carry):
        high = z + 1 + step
        low = z - 1 - step
        pl.when(high < nz)(lambda: compute(high))
        pl.when(jnp.logical_and(high < nz, z == 0))(lambda: finish(0, high, False))
        relay(step + 1)
        pl.when(low >= 0)(lambda: compute(low))
        pl.when(jnp.logical_and(low >= 0, z == nz - 1))(lambda: finish(1, low, False))
        return carry

    lax.fori_loop(0, nz - 1, return_step, 0)
    far = cached(mate)
    save(z, 0, far[:1])
    over[0, z] = pack_partial(far[1:])
    send_over(z).start()
    save(z, 1, merge(load(z, 1, 5), cached(me)))

    def merge_step(step, carry):
        distance = nz - 2 - step
        high = z + distance
        low = z - distance
        pl.when(jnp.logical_and(high < nz, not_first))(lambda: finish(0, high, True))
        pl.when(jnp.logical_and(low >= 0, not_last))(lambda: finish(1, low, True))
        return carry

    lax.fori_loop(0, nz - 2, merge_step, 0)

    def gather_in(buffer, kind, way, condition, held):
        copy, slot = arriving(buffer, kind, way, z)
        pl.when(condition)(lambda: copy.wait_recv())

        @pl.when(jnp.logical_not(condition))
        def _():
            buffer[slot] = jnp.zeros(buffer.shape[1:], BF16)

        arrived = unpack_partial(buffer[slot])
        arrived = [(numer, jnp.where(condition, top, NEGATIVE), total) for numer, top, total in arrived]
        return merge(held, arrived)

    firsts = load(z, 0, 2)
    firsts = gather_in(first_way, 0, 0, not_first, firsts)
    firsts = gather_in(first_way, 0, 1, not_last, firsts)
    cross[0] = pack_partial(firsts[:1])
    to_mate = remote(cross.at[0], cross.at[1], xsend, xrecv, req=mate)
    to_mate.start()

    remote(wo_all.at[y_mate], wo_all.at[y_mate], tsend.at[0], trecv.at[0], tp=y_mate).wait_recv()
    wo_far = remote(wo_all.at[y_mate], wo_all.at[y_mate], tsend.at[2], trecv.at[2], tp=core_mate)
    wo_far.start()

    loads[3].wait()
    down_t[...] = down_v[...].T
    send_over(z).wait_recv()
    rest = merge(load(z, 2, 5), unpack_partial(over[1, z]))
    rest = gather_in(rest_way, 1, 0, not_first, rest)
    rest = gather_in(rest_way, 1, 1, not_last, rest)
    to_mate.wait_recv()
    mine = merge(firsts[1:], unpack_partial(cross[1])) + rest
    att[tp] = jnp.concatenate([(numer / total).astype(BF16) for numer, _, total in mine], axis=0)

    att_y = remote(att.at[tp], att.at[tp], tsend.at[3], trecv.at[3], tp=y_mate)
    att_core = remote(att.at[tp], att.at[tp], tsend.at[4], trecv.at[4], tp=core_mate)
    att_y.start()
    att_core.start()

    def projected(index):
        return matmul(att[index].T, wo_all[index])

    terms = projected(tp)
    remote(wo_all.at[core_mate], wo_all.at[core_mate], tsend.at[1], trecv.at[1], tp=core_mate).wait_recv()
    remote(att.at[core_mate], att.at[core_mate], tsend.at[4], trecv.at[4], tp=core_mate).wait_recv()
    terms = terms + projected(core_mate)
    remote(att.at[y_mate], att.at[y_mate], tsend.at[3], trecv.at[3], tp=y_mate).wait_recv()
    att_far = remote(att.at[y_mate], att.at[y_mate], tsend.at[5], trecv.at[5], tp=core_mate)
    att_far.start()
    terms = terms + projected(y_mate)
    diagonal = (core_mate + 2) % 4
    remote(wo_all.at[diagonal], wo_all.at[diagonal], tsend.at[2], trecv.at[2], tp=core_mate).wait_recv()
    remote(att.at[diagonal], att.at[diagonal], tsend.at[5], trecv.at[5], tp=core_mate).wait_recv()
    terms = terms + projected(diagonal)

    middle = (tokens[...].astype(F32) + terms).astype(BF16).astype(F32)
    normed_middle = normalize(middle, gain_f[...].astype(F32)[None, :])
    loads[4].wait()
    gate = matmul_rows(up_v[...], normed_middle)
    hidden_t = (gate / (1.0 + jnp.exp(-gate))).astype(BF16)

    def down_part(index):
        return matmul(down_t[pl.ds(pl.multiple_of(index * WIDTH, 16), WIDTH)], hidden_t)

    core_out[0] = down_part(diagonal).astype(BF16)
    core_out[1] = down_part(core_mate).astype(BF16)
    fold = remote(core_out, core_in, tsend.at[6], trecv.at[6], tp=core_mate)
    fold.start()
    far_part = down_part(y_mate)
    near_part = down_part(tp)
    mid_t[...] = middle.T
    near_part = near_part + mid_t[pl.ds(pl.multiple_of(tp * WIDTH, 16), WIDTH)]
    fold.wait_recv()
    y_out[...] = (far_part + core_in[0].astype(F32)).astype(BF16)
    swap = remote(y_out, y_in, tsend.at[7], trecv.at[7], tp=y_mate)
    swap.start()
    near_part = near_part + core_in[1].astype(F32)
    lane = lax.broadcasted_iota(jnp.int32, (WIDTH, ROWS), 1)
    live = jnp.where(lane < SLOT, length[me * R_DEV], length[me * R_DEV + 1])
    swap.wait_recv()
    layer = near_part + y_in[...].astype(F32)
    out[...] = jnp.where(lane % SLOT < live, layer, 0.0).astype(BF16)

    over_whole.wait_send()

    def sent_step(plane, carry):
        pl.when(plane != z)(lambda: over_late(plane).wait_send())

        @pl.when(jnp.logical_and(not_last, plane <= z))
        def _():
            up_whole(plane).wait_send()
            up_early(plane).wait_send()

        @pl.when(jnp.logical_and(not_first, plane >= z))
        def _():
            down_whole(plane).wait_send()
            down_early(plane).wait_send()

        send_over(plane).wait_send()

        for kind, buffer in ((0, first_way), (1, rest_way)):
            pl.when(plane > z)(lambda: passing(buffer, kind, 0, plane).wait_send())
            pl.when(plane < z)(lambda: passing(buffer, kind, 1, plane).wait_send())

        return carry

    lax.fori_loop(0, nz, sent_step, 0)
    for copy in (to_mate, wo_y, wo_core, wo_far, att_y, att_core, att_far, fold, swap):
        copy.wait_send()


def per_device(
    tokens,
    attention_gain,
    feedforward_gain,
    query_weight,
    key_weight,
    value_weight,
    out_weight,
    up_weight,
    down_weight,
    cache_keys,
    cache_values,
    request_prefix,
    suffix_length,
):
    owners = lax.axis_size("req")
    nz = owners // 2
    rows, model = tokens.shape
    prefixes = cache_keys.shape[1]
    dma = pltpu.SemaphoreType.DMA
    vmem = pl.BlockSpec(memory_space=pltpu.VMEM)
    smem = pl.BlockSpec(memory_space=pltpu.SMEM)
    away = pl.BlockSpec(memory_space=pl.ANY)
    return pl.pallas_call(
        functools.partial(kernel, nz),
        out_shape=jax.ShapeDtypeStruct((WIDTH, rows), BF16),
        in_specs=[vmem] * 6 + [away] * 5 + [smem] * 2,
        out_specs=vmem,
        scratch_shapes=[
            pltpu.VMEM((owners, WIDTH, ROWS), BF16),
            pltpu.VMEM((prefixes, PG, WIDTH), BF16),
            pltpu.VMEM((prefixes, PG, WIDTH), BF16),
            pltpu.VMEM((4, WIDTH, model), BF16),
            pltpu.VMEM((WIDTH, model), BF16),
            pltpu.VMEM((WIDTH, model), BF16),
            pltpu.VMEM((model, WIDTH), BF16),
            pltpu.VMEM((ROWS, WIDTH), BF16),
            pltpu.VMEM((WIDTH, ROWS), BF16),
            pltpu.VMEM((prefixes, WIDTH, PG), BF16),
            pltpu.VMEM((nz, FIRST + WIDTH, ROWS), F32),
            pltpu.VMEM((nz, STATS, ROWS), F32),
            pltpu.VMEM((nz + 1, REST + STATS, ROWS), BF16),
            pltpu.VMEM((nz + 1, 2 * FIRST + STATS, ROWS), BF16),
            pltpu.VMEM((2, nz, REST + STATS, ROWS), BF16),
            pltpu.VMEM((2, FIRST + STATS, ROWS), BF16),
            pltpu.VMEM((4, WIDTH, ROWS), BF16),
            pltpu.VMEM((2, WIDTH, ROWS), BF16),
            pltpu.VMEM((2, WIDTH, ROWS), BF16),
            pltpu.VMEM((WIDTH, ROWS), BF16),
            pltpu.VMEM((WIDTH, ROWS), BF16),
            pltpu.VMEM((model, ROWS), F32),
            dma((5,)),
            dma((5, nz)),
            dma((3, nz)),
            dma((2, nz + 1)),
            dma((2, nz + 1)),
            dma,
            dma,
            dma((8,)),
            dma((8,)),
            dma((nz,)),
            dma((nz,)),
        ],
        compiler_params=pltpu.CompilerParams(
            collective_id=0, has_side_effects=True, vmem_limit_bytes=60 * 1024 * 1024
        ),
    )(
        tokens,
        attention_gain,
        feedforward_gain,
        query_weight.T,
        key_weight.T,
        value_weight.T,
        out_weight,
        up_weight.T,
        down_weight,
        cache_keys[0],
        cache_values[0],
        request_prefix,
        suffix_length,
    ).T


def solution(mesh):
    in_specs = (
        P("req", None),
        P(),
        P(),
        P(None, "tp"),
        P(None, "tp"),
        P(None, "tp"),
        P("tp", None),
        P(None, "tp"),
        P("tp", None),
        P("req", None, None, "tp"),
        P("req", None, None, "tp"),
        P(),
        P(),
    )
    out_specs = P("req", "tp")
    return jax.shard_map(
        per_device, mesh=mesh, in_specs=in_specs, out_specs=out_specs, check_vma=False
    )
```

```python
import functools
import math

import jax
import jax.numpy as jnp
from jax import lax
from jax.experimental import pallas as pl
from jax.experimental.pallas import tpu as pltpu
from jax.sharding import PartitionSpec as P

HDIM = 80
SLOT = 128
R_DEV = 2
PG = 192
LOCAL_HEADS = 4
WIDTH = HDIM * LOCAL_HEADS
ROWS = R_DEV * SLOT
STATS = 16
FIRST = HDIM
REST = WIDTH - HDIM

EPSILON = 1e-06
NEGATIVE = -1e30
MESH = pl.DeviceIdType.MESH
F32 = jnp.float32
BF16 = jnp.bfloat16


def normalize(floats, gain):
    mean_square = jnp.mean(floats * floats, axis=-1, keepdims=True)
    return (floats * lax.rsqrt(mean_square + EPSILON) * gain).astype(BF16)


def matmul(left, right):
    return jnp.dot(left, right, preferred_element_type=F32)


def matmul_rows(left, right):
    return lax.dot_general(left, right, (((1,), (1,)), ((), ())), preferred_element_type=F32)


def head_rows(values, head):
    return values[head * HDIM : (head + 1) * HDIM]


def request_partial(query_t, keys, values_t, causal):
    none = jnp.zeros((HDIM, SLOT), BF16)
    partial = []
    for pair, (start, stop) in enumerate(((0, 256), (128, WIDTH))):
        first, second = head_rows(query_t, 2 * pair), head_rows(query_t, 2 * pair + 1)
        above = 2 * pair * HDIM - start
        below = stop - start - above - 2 * HDIM
        blocks = [jnp.zeros((above, 2 * SLOT), BF16)] if above else []
        blocks.append(jnp.concatenate([first, none], axis=1))
        blocks.append(jnp.concatenate([none, second], axis=1))
        if below:
            blocks.append(jnp.zeros((below, 2 * SLOT), BF16))
        scores = matmul(keys[:, start:stop], jnp.concatenate(blocks, axis=0)) * (1.0 / math.sqrt(HDIM))
        if causal:
            key_row = lax.broadcasted_iota(jnp.int32, scores.shape, 0)
            query_row = lax.broadcasted_iota(jnp.int32, scores.shape, 1) % SLOT
            scores = jnp.where(key_row <= query_row, scores, NEGATIVE)
        top = jnp.max(scores, axis=0, keepdims=True)
        if not causal:
            top = top.astype(BF16).astype(F32)
        weights = jnp.exp(scores - top)
        total = jnp.sum(weights, axis=0, keepdims=True)
        numer = matmul(values_t[2 * pair * HDIM : 2 * (pair + 1) * HDIM], weights.astype(BF16))
        partial.append((numer[:HDIM, :SLOT], top[:, :SLOT], total[:, :SLOT]))
        partial.append((numer[HDIM:, SLOT:], top[:, SLOT:], total[:, SLOT:]))
    return partial


def both_requests(first, second):
    return [
        tuple(jnp.concatenate([a, b], axis=1) for a, b in zip(first[h], second[h]))
        for h in range(LOCAL_HEADS)
    ]


def merge(one, other):
    merged = []
    for (numer_a, top_a, total_a), (numer_b, top_b, total_b) in zip(one, other):
        top = jnp.maximum(top_a, top_b)
        factor_a = jnp.exp(top_a - top)
        factor_b = jnp.exp(top_b - top)
        merged.append(
            (
                numer_a * factor_a + numer_b * factor_b,
                top,
                total_a * factor_a + total_b * factor_b,
            )
        )
    return merged


def pack_partial(partial):
    heads = len(partial)
    shares = [(numer / total).astype(BF16) for numer, _, total in partial]
    tops = [top for _, top, _ in partial]
    whole = [total.astype(BF16).astype(F32) for _, _, total in partial]
    rest = [total - high for (_, _, total), high in zip(partial, whole)]
    pad = [jnp.zeros((STATS - 3 * heads, ROWS), F32)]
    stats = jnp.concatenate(tops + whole + rest + pad, axis=0).astype(BF16)
    return jnp.concatenate(shares + [stats], axis=0)


def unpack_partial(block):
    heads = (block.shape[0] - STATS) // HDIM
    stats = block[heads * HDIM :].astype(F32)
    partial = []
    for h in range(heads):
        top = stats[h : h + 1]
        total = stats[heads + h : heads + h + 1]
        total = total + stats[2 * heads + h : 2 * heads + h + 1]
        partial.append((head_rows(block, h).astype(F32) * total, top, total))
    return partial


def kernel(
    nz,
    tokens,
    gain_a,
    gain_f,
    wq,
    wk,
    wv,
    wo,
    wup,
    wdown,
    cache_k,
    cache_v,
    prefix,
    length,
    out,
    qbuf,
    kbuf,
    vbuf,
    wo_all,
    up_v,
    down_v,
    down_t,
    own_k,
    own_v,
    cache_vt,
    numers,
    stats,
    rest_way,
    first_way,
    over,
    cross,
    att,
    core_out,
    core_in,
    y_out,
    y_in,
    mid_t,
    local_sem,
    qsend,
    qrecv,
    psend,
    precv,
    xsend,
    xrecv,
    tsend,
    trecv,
    osend,
    orecv,
    wk_v,
    wv_v,
):
    me = lax.axis_index("req")
    tp = lax.axis_index("tp")
    z = me // 2
    x = me % 2
    mate = z * 2 + 1 - x
    core_mate = tp + 1 - 2 * (tp % 2)
    y_mate = (tp + 2) % 4
    not_first = z > 0
    not_last = z < nz - 1

    def remote(source, target, send_sem, recv_sem, **where):
        return pltpu.make_async_remote_copy(
            src_ref=source,
            dst_ref=target,
            send_sem=send_sem,
            recv_sem=recv_sem,
            device_id=where,
            device_id_type=MESH,
        )

    barrier = pltpu.get_barrier_semaphore()

    def greet(**where):
        pl.semaphore_signal(barrier, inc=1, device_id=where, device_id_type=MESH)

    greet(req=mate)
    greet(tp=core_mate)
    greet(tp=y_mate)
    pl.when(not_first)(lambda: greet(req=me - 2))
    pl.when(not_last)(lambda: greet(req=me + 2))

    loads = [
        pltpu.make_async_copy(source, target, local_sem.at[i])
        for i, (source, target) in enumerate(
            [(wo, wo_all.at[tp]), (cache_k, kbuf), (cache_v, vbuf), (wdown, down_v), (wup, up_v), (wk, wk_v), (wv, wv_v)]
        )
    ]
    for load in loads:
        load.start()

    normed = normalize(tokens[...].astype(F32), gain_a[...].astype(F32)[None, :])
    qbuf[me] = matmul_rows(wq[...], normed).astype(BF16)

    pl.semaphore_wait(barrier, 3 + jnp.where(not_first, 1, 0) + jnp.where(not_last, 1, 0))

    def whole(plane, column):
        return qbuf.at[plane * 2 + column]

    def early(plane, column):
        return qbuf.at[plane * 2 + column, pl.ds(0, FIRST)]

    def late(plane, column):
        return qbuf.at[plane * 2 + column, pl.ds(FIRST, REST)]

    def up_whole(plane):
        return remote(whole(plane, x), whole(plane, x), qsend.at[0, plane], qrecv.at[0, plane], req=me + 2)

    def up_early(plane):
        return remote(early(plane, 1 - x), early(plane, 1 - x), qsend.at[1, plane], qrecv.at[1, plane], req=me + 2)

    def down_whole(plane):
        return remote(whole(plane, x), whole(plane, x), qsend.at[2, plane], qrecv.at[0, plane], req=me - 2)

    def down_early(plane):
        return remote(early(plane, 1 - x), early(plane, 1 - x), qsend.at[3, plane], qrecv.at[1, plane], req=me - 2)

    def over_late(plane):
        return remote(late(plane, x), late(plane, x), qsend.at[4, plane], qrecv.at[2, plane], req=mate)

    over_whole = remote(whole(z, x), whole(z, x), qsend.at[4, z], qrecv.at[2, z], req=mate)
    got_whole = remote(whole(z, 1 - x), whole(z, 1 - x), qsend.at[4, z], qrecv.at[2, z], req=mate)

    over_whole.start()
    pl.when(not_last)(lambda: up_whole(z).start())
    pl.when(not_first)(lambda: down_whole(z).start())

    loads[0].wait()
    wo_y = remote(wo_all.at[tp], wo_all.at[tp], tsend.at[0], trecv.at[0], tp=y_mate)
    wo_core = remote(wo_all.at[tp], wo_all.at[tp], tsend.at[1], trecv.at[1], tp=core_mate)
    wo_y.start()
    wo_core.start()

    got_whole.wait_recv()
    pl.when(not_last)(lambda: up_early(z).start())
    pl.when(not_first)(lambda: down_early(z).start())

    loads[5].wait()
    loads[6].wait()
    own_k[...] = matmul_rows(normed, wk_v[...]).astype(BF16)
    own_v[...] = matmul_rows(wv_v[...], normed).astype(BF16)

    def save(plane, start, partial):
        for place, (numer, top, total) in enumerate(partial, start):
            numers[plane, pl.ds(place * HDIM, HDIM)] = numer
            stats[plane, pl.ds(place, 1)] = top
            stats[plane, pl.ds(8 + place, 1)] = total

    def load(plane, start, stop):
        held = stats[plane]
        return [
            (
                numers[plane, pl.ds(place * HDIM, HDIM)],
                held[place : place + 1],
                held[8 + place : 9 + place],
            )
            for place in range(start, stop)
        ]

    def cached(target):
        queries = qbuf[target]
        parts = []
        for j in range(R_DEV):
            chosen = prefix[target * R_DEV + j]
            parts.append(
                request_partial(
                    queries[:, j * SLOT : (j + 1) * SLOT], kbuf[chosen], cache_vt[chosen], False
                )
            )
        return both_requests(*parts)

    save(
        z,
        1,
        both_requests(
            *[
                request_partial(
                    qbuf[me, :, pl.ds(j * SLOT, SLOT)],
                    own_k[pl.ds(j * SLOT, SLOT), :],
                    own_v[:, pl.ds(j * SLOT, SLOT)],
                    True,
                )
                for j in range(R_DEV)
            ]
        ),
    )

    def relay(step):
        below = z - 1 - step
        above = z + 1 + step

        @pl.when(below >= 0)
        def _():
            up_whole(below).wait_recv()
            pl.when(not_last)(lambda: up_whole(below).start())
            over_late(below).start()

        @pl.when(above < nz)
        def _():
            down_whole(above).wait_recv()
            pl.when(not_first)(lambda: down_whole(above).start())
            over_late(above).start()

        @pl.when(below >= 0)
        def _():
            up_early(below).wait_recv()
            pl.when(not_last)(lambda: up_early(below).start())

        @pl.when(above < nz)
        def _():
            down_early(above).wait_recv()
            pl.when(not_first)(lambda: down_early(above).start())

    def turn(index, carry):
        cache_vt[index] = vbuf[index].T
        return carry

    relay(0)
    loads[1].wait()
    loads[2].wait()
    lax.fori_loop(0, vbuf.shape[0], turn, 0)

    def send_over(plane):
        return remote(over.at[0, plane], over.at[1, plane], osend.at[plane], orecv.at[plane], req=mate)

    def passing(buffer, kind, way, plane):
        there = me + 2 - 4 * way
        here_slot = jnp.where(jnp.logical_and(way == 1, plane == z), nz, plane)
        there_slot = jnp.where(jnp.logical_and(way == 1, plane == z - 1), nz, plane)
        return remote(
            buffer.at[here_slot],
            buffer.at[there_slot],
            psend.at[kind, here_slot],
            precv.at[kind, there_slot],
            req=there,
        )

    def arriving(buffer, kind, way, plane):
        slot = jnp.where(jnp.logical_and(way == 1, plane == z), nz, plane)
        copy = remote(
            buffer.at[slot], buffer.at[slot], psend.at[kind, slot], precv.at[kind, slot], req=me - 2 + 4 * way
        )
        return copy, slot

    def compute(plane):
        remote(late(plane, 1 - x), late(plane, 1 - x), qsend.at[4, plane], qrecv.at[2, plane], req=mate).wait_recv()
        far = cached(plane * 2 + 1 - x)
        save(plane, 0, far[:1])
        over[0, plane] = pack_partial(far[1:])
        send_over(plane).start()
        save(plane, 1, cached(plane * 2 + x))

    def finish(way, plane, has_source):
        def pass_on(buffer, kind, partial):
            if has_source:
                copy, slot = arriving(buffer, kind, way, plane)
                copy.wait_recv()
                partial = merge(partial, unpack_partial(buffer[slot]))
            buffer[plane] = pack_partial(partial)
            passing(buffer, kind, way, plane).start()

        pass_on(first_way, 0, load(plane, 0, 2))
        send_over(plane).wait_recv()
        pass_on(rest_way, 1, merge(load(plane, 2, 5), unpack_partial(over[1, plane])))

    def return_step(step, carry):
        high = z + 1 + step
        low = z - 1 - step
        pl.when(high < nz)(lambda: compute(high))
        pl.when(jnp.logical_and(high < nz, z == 0))(lambda: finish(0, high, False))
        relay(step + 1)
        pl.when(low >= 0)(lambda: compute(low))
        pl.when(jnp.logical_and(low >= 0, z == nz - 1))(lambda: finish(1, low, False))
        return carry

    lax.fori_loop(0, nz - 1, return_step, 0)
    def merge_step(step, carry):
        distance = nz - 2 - step
        high = z + distance
        low = z - distance
        pl.when(jnp.logical_and(high < nz, not_first))(lambda: finish(0, high, True))
        pl.when(jnp.logical_and(low >= 0, not_last))(lambda: finish(1, low, True))

        @pl.when(step == 0)
        def _():
            far = cached(mate)
            save(z, 0, far[:1])
            over[0, z] = pack_partial(far[1:])
            send_over(z).start()
            save(z, 1, merge(load(z, 1, 5), cached(me)))

        return carry

    lax.fori_loop(0, nz - 2, merge_step, 0)

    def gather_in(buffer, kind, way, condition, held):
        copy, slot = arriving(buffer, kind, way, z)
        pl.when(condition)(lambda: copy.wait_recv())

        @pl.when(jnp.logical_not(condition))
        def _():
            buffer[slot] = jnp.zeros(buffer.shape[1:], BF16)

        arrived = unpack_partial(buffer[slot])
        arrived = [(numer, jnp.where(condition, top, NEGATIVE), total) for numer, top, total in arrived]
        return merge(held, arrived)

    firsts = load(z, 0, 2)
    firsts = gather_in(first_way, 0, 0, not_first, firsts)
    firsts = gather_in(first_way, 0, 1, not_last, firsts)
    cross[0] = pack_partial(firsts[:1])
    to_mate = remote(cross.at[0], cross.at[1], xsend, xrecv, req=mate)
    to_mate.start()

    remote(wo_all.at[y_mate], wo_all.at[y_mate], tsend.at[0], trecv.at[0], tp=y_mate).wait_recv()
    wo_far = remote(wo_all.at[y_mate], wo_all.at[y_mate], tsend.at[2], trecv.at[2], tp=core_mate)
    wo_far.start()

    loads[3].wait()
    down_t[...] = down_v[...].T
    send_over(z).wait_recv()
    rest = merge(load(z, 2, 5), unpack_partial(over[1, z]))
    rest = gather_in(rest_way, 1, 0, not_first, rest)
    rest = gather_in(rest_way, 1, 1, not_last, rest)
    to_mate.wait_recv()
    mine = merge(firsts[1:], unpack_partial(cross[1])) + rest
    att[tp] = jnp.concatenate([(numer / total).astype(BF16) for numer, _, total in mine], axis=0)

    att_y = remote(att.at[tp], att.at[tp], tsend.at[3], trecv.at[3], tp=y_mate)
    att_core = remote(att.at[tp], att.at[tp], tsend.at[4], trecv.at[4], tp=core_mate)
    att_y.start()
    att_core.start()

    def projected(index):
        return matmul(att[index].T, wo_all[index])

    terms = projected(tp)
    remote(wo_all.at[core_mate], wo_all.at[core_mate], tsend.at[1], trecv.at[1], tp=core_mate).wait_recv()
    remote(att.at[core_mate], att.at[core_mate], tsend.at[4], trecv.at[4], tp=core_mate).wait_recv()
    terms = terms + projected(core_mate)
    remote(att.at[y_mate], att.at[y_mate], tsend.at[3], trecv.at[3], tp=y_mate).wait_recv()
    att_far = remote(att.at[y_mate], att.at[y_mate], tsend.at[5], trecv.at[5], tp=core_mate)
    att_far.start()
    terms = terms + projected(y_mate)
    diagonal = (core_mate + 2) % 4
    remote(wo_all.at[diagonal], wo_all.at[diagonal], tsend.at[2], trecv.at[2], tp=core_mate).wait_recv()
    remote(att.at[diagonal], att.at[diagonal], tsend.at[5], trecv.at[5], tp=core_mate).wait_recv()
    terms = terms + projected(diagonal)

    middle = (tokens[...].astype(F32) + terms).astype(BF16).astype(F32)
    normed_middle = normalize(middle, gain_f[...].astype(F32)[None, :])
    loads[4].wait()
    gate = matmul_rows(up_v[...], normed_middle)
    hidden_t = (gate / (1.0 + jnp.exp(-gate))).astype(BF16)

    def down_part(index):
        return matmul(down_t[pl.ds(pl.multiple_of(index * WIDTH, 16), WIDTH)], hidden_t)

    core_out[0] = down_part(diagonal).astype(BF16)
    core_out[1] = down_part(core_mate).astype(BF16)
    fold = remote(core_out, core_in, tsend.at[6], trecv.at[6], tp=core_mate)
    fold.start()
    far_part = down_part(y_mate)
    near_part = down_part(tp)
    mid_t[...] = middle.T
    near_part = near_part + mid_t[pl.ds(pl.multiple_of(tp * WIDTH, 16), WIDTH)]
    fold.wait_recv()
    y_out[...] = (far_part + core_in[0].astype(F32)).astype(BF16)
    swap = remote(y_out, y_in, tsend.at[7], trecv.at[7], tp=y_mate)
    swap.start()
    near_part = near_part + core_in[1].astype(F32)
    lane = lax.broadcasted_iota(jnp.int32, (WIDTH, ROWS), 1)
    live = jnp.where(lane < SLOT, length[me * R_DEV], length[me * R_DEV + 1])
    swap.wait_recv()
    layer = near_part + y_in[...].astype(F32)
    out[...] = jnp.where(lane % SLOT < live, layer, 0.0).astype(BF16)

    over_whole.wait_send()

    def sent_step(plane, carry):
        pl.when(plane != z)(lambda: over_late(plane).wait_send())

        @pl.when(jnp.logical_and(not_last, plane <= z))
        def _():
            up_whole(plane).wait_send()
            up_early(plane).wait_send()

        @pl.when(jnp.logical_and(not_first, plane >= z))
        def _():
            down_whole(plane).wait_send()
            down_early(plane).wait_send()

        send_over(plane).wait_send()

        for kind, buffer in ((0, first_way), (1, rest_way)):
            pl.when(plane > z)(lambda: passing(buffer, kind, 0, plane).wait_send())
            pl.when(plane < z)(lambda: passing(buffer, kind, 1, plane).wait_send())

        return carry

    lax.fori_loop(0, nz, sent_step, 0)
    for copy in (to_mate, wo_y, wo_core, wo_far, att_y, att_core, att_far, fold, swap):
        copy.wait_send()


def per_device(
    tokens,
    attention_gain,
    feedforward_gain,
    query_weight,
    key_weight,
    value_weight,
    out_weight,
    up_weight,
    down_weight,
    cache_keys,
    cache_values,
    request_prefix,
    suffix_length,
):
    owners = lax.axis_size("req")
    nz = owners // 2
    rows, model = tokens.shape
    prefixes = cache_keys.shape[1]
    dma = pltpu.SemaphoreType.DMA
    vmem = pl.BlockSpec(memory_space=pltpu.VMEM)
    smem = pl.BlockSpec(memory_space=pltpu.SMEM)
    away = pl.BlockSpec(memory_space=pl.ANY)
    return pl.pallas_call(
        functools.partial(kernel, nz),
        out_shape=jax.ShapeDtypeStruct((WIDTH, rows), BF16),
        in_specs=[vmem] * 4 + [away] * 7 + [smem] * 2,
        out_specs=vmem,
        scratch_shapes=[
            pltpu.VMEM((owners, WIDTH, ROWS), BF16),
            pltpu.VMEM((prefixes, PG, WIDTH), BF16),
            pltpu.VMEM((prefixes, PG, WIDTH), BF16),
            pltpu.VMEM((4, WIDTH, model), BF16),
            pltpu.VMEM((WIDTH, model), BF16),
            pltpu.VMEM((WIDTH, model), BF16),
            pltpu.VMEM((model, WIDTH), BF16),
            pltpu.VMEM((ROWS, WIDTH), BF16),
            pltpu.VMEM((WIDTH, ROWS), BF16),
            pltpu.VMEM((prefixes, WIDTH, PG), BF16),
            pltpu.VMEM((nz, FIRST + WIDTH, ROWS), F32),
            pltpu.VMEM((nz, STATS, ROWS), F32),
            pltpu.VMEM((nz + 1, REST + STATS, ROWS), BF16),
            pltpu.VMEM((nz + 1, 2 * FIRST + STATS, ROWS), BF16),
            pltpu.VMEM((2, nz, REST + STATS, ROWS), BF16),
            pltpu.VMEM((2, FIRST + STATS, ROWS), BF16),
            pltpu.VMEM((4, WIDTH, ROWS), BF16),
            pltpu.VMEM((2, WIDTH, ROWS), BF16),
            pltpu.VMEM((2, WIDTH, ROWS), BF16),
            pltpu.VMEM((WIDTH, ROWS), BF16),
            pltpu.VMEM((WIDTH, ROWS), BF16),
            pltpu.VMEM((model, ROWS), F32),
            dma((7,)),
            dma((5, nz)),
            dma((3, nz)),
            dma((2, nz + 1)),
            dma((2, nz + 1)),
            dma,
            dma,
            dma((8,)),
            dma((8,)),
            dma((nz,)),
            dma((nz,)),
            pltpu.VMEM((WIDTH, model), BF16),
            pltpu.VMEM((WIDTH, model), BF16),
        ],
        compiler_params=pltpu.CompilerParams(
            collective_id=0, has_side_effects=True, vmem_limit_bytes=60 * 1024 * 1024
        ),
    )(
        tokens,
        attention_gain,
        feedforward_gain,
        query_weight.T,
        key_weight.T,
        value_weight.T,
        out_weight,
        up_weight.T,
        down_weight,
        cache_keys[0],
        cache_values[0],
        request_prefix,
        suffix_length,
    ).T


def solution(mesh):
    in_specs = (
        P("req", None),
        P(),
        P(),
        P(None, "tp"),
        P(None, "tp"),
        P(None, "tp"),
        P("tp", None),
        P(None, "tp"),
        P("tp", None),
        P("req", None, None, "tp"),
        P("req", None, None, "tp"),
        P(),
        P(),
    )
    out_specs = P("req", "tp")
    return jax.shard_map(
        per_device, mesh=mesh, in_specs=in_specs, out_specs=out_specs, check_vma=False
    )
```

```python
import functools
import math

import jax
import jax.numpy as jnp
from jax import lax
from jax.experimental import pallas as pl
from jax.experimental.pallas import tpu as pltpu
from jax.sharding import PartitionSpec as P

HDIM = 80
SLOT = 128
R_DEV = 2
PG = 192
LOCAL_HEADS = 4
WIDTH = HDIM * LOCAL_HEADS
ROWS = R_DEV * SLOT
STATS = 16
FIRST = HDIM
REST = WIDTH - HDIM

EPSILON = 1e-06
NEGATIVE = -1e30
MESH = pl.DeviceIdType.MESH
F32 = jnp.float32
BF16 = jnp.bfloat16


def normalize(floats, gain):
    mean_square = jnp.mean(floats * floats, axis=-1, keepdims=True)
    return (floats * lax.rsqrt(mean_square + EPSILON) * gain).astype(BF16)


def matmul(left, right):
    return jnp.dot(left, right, preferred_element_type=F32)


def matmul_rows(left, right):
    return lax.dot_general(left, right, (((1,), (1,)), ((), ())), preferred_element_type=F32)


def head_rows(values, head):
    return values[head * HDIM : (head + 1) * HDIM]


def request_partial(query_t, keys, values_t, causal):
    none = jnp.zeros((HDIM, SLOT), BF16)
    partial = []
    for pair, (start, stop) in enumerate(((0, 256), (128, WIDTH))):
        first, second = head_rows(query_t, 2 * pair), head_rows(query_t, 2 * pair + 1)
        above = 2 * pair * HDIM - start
        below = stop - start - above - 2 * HDIM
        blocks = [jnp.zeros((above, 2 * SLOT), BF16)] if above else []
        blocks.append(jnp.concatenate([first, none], axis=1))
        blocks.append(jnp.concatenate([none, second], axis=1))
        if below:
            blocks.append(jnp.zeros((below, 2 * SLOT), BF16))
        scores = matmul(keys[:, start:stop], jnp.concatenate(blocks, axis=0)) * (1.0 / math.sqrt(HDIM))
        if causal:
            key_row = lax.broadcasted_iota(jnp.int32, scores.shape, 0)
            query_row = lax.broadcasted_iota(jnp.int32, scores.shape, 1) % SLOT
            scores = jnp.where(key_row <= query_row, scores, NEGATIVE)
        top = jnp.max(scores, axis=0, keepdims=True)
        if not causal:
            top = top.astype(BF16).astype(F32)
        weights = jnp.exp(scores - top)
        total = jnp.sum(weights, axis=0, keepdims=True)
        numer = matmul(values_t[2 * pair * HDIM : 2 * (pair + 1) * HDIM], weights.astype(BF16))
        partial.append((numer[:HDIM, :SLOT], top[:, :SLOT], total[:, :SLOT]))
        partial.append((numer[HDIM:, SLOT:], top[:, SLOT:], total[:, SLOT:]))
    return partial


def both_requests(first, second):
    return [
        tuple(jnp.concatenate([a, b], axis=1) for a, b in zip(first[h], second[h]))
        for h in range(LOCAL_HEADS)
    ]


def merge(one, other):
    merged = []
    for (numer_a, top_a, total_a), (numer_b, top_b, total_b) in zip(one, other):
        top = jnp.maximum(top_a, top_b)
        factor_a = jnp.exp(top_a - top)
        factor_b = jnp.exp(top_b - top)
        merged.append(
            (
                numer_a * factor_a + numer_b * factor_b,
                top,
                total_a * factor_a + total_b * factor_b,
            )
        )
    return merged


def pack_partial(partial):
    heads = len(partial)
    shares = [(numer / total).astype(BF16) for numer, _, total in partial]
    tops = [top for _, top, _ in partial]
    whole = [total.astype(BF16).astype(F32) for _, _, total in partial]
    rest = [total - high for (_, _, total), high in zip(partial, whole)]
    pad = [jnp.zeros((STATS - 3 * heads, ROWS), F32)]
    stats = jnp.concatenate(tops + whole + rest + pad, axis=0).astype(BF16)
    return jnp.concatenate(shares + [stats], axis=0)


def unpack_partial(block):
    heads = (block.shape[0] - STATS) // HDIM
    stats = block[heads * HDIM :].astype(F32)
    partial = []
    for h in range(heads):
        top = stats[h : h + 1]
        total = stats[heads + h : heads + h + 1]
        total = total + stats[2 * heads + h : 2 * heads + h + 1]
        partial.append((head_rows(block, h).astype(F32) * total, top, total))
    return partial


def kernel(
    nz,
    tokens,
    gain_a,
    gain_f,
    wq,
    wk,
    wv,
    wo,
    wup,
    wdown,
    cache_k,
    cache_v,
    prefix,
    length,
    out,
    qbuf,
    kbuf,
    vbuf,
    wo_all,
    up_v,
    down_v,
    down_t,
    own_k,
    own_v,
    cache_vt,
    numers,
    stats,
    rest_way,
    first_way,
    over,
    cross,
    att,
    core_out,
    core_in,
    y_out,
    y_in,
    mid_t,
    local_sem,
    qsend,
    qrecv,
    psend,
    precv,
    xsend,
    xrecv,
    tsend,
    trecv,
    osend,
    orecv,
    wk_v,
    wv_v,
):
    me = lax.axis_index("req")
    tp = lax.axis_index("tp")
    z = me // 2
    x = me % 2
    mate = z * 2 + 1 - x
    core_mate = tp + 1 - 2 * (tp % 2)
    y_mate = (tp + 2) % 4
    not_first = z > 0
    not_last = z < nz - 1

    def remote(source, target, send_sem, recv_sem, **where):
        return pltpu.make_async_remote_copy(
            src_ref=source,
            dst_ref=target,
            send_sem=send_sem,
            recv_sem=recv_sem,
            device_id=where,
            device_id_type=MESH,
        )

    barrier = pltpu.get_barrier_semaphore()

    def greet(**where):
        pl.semaphore_signal(barrier, inc=1, device_id=where, device_id_type=MESH)

    greet(req=mate)
    greet(tp=core_mate)
    greet(tp=y_mate)
    pl.when(not_first)(lambda: greet(req=me - 2))
    pl.when(not_last)(lambda: greet(req=me + 2))
    span = 2 * (nz - 1)
    pl.when(jnp.logical_not(not_first))(lambda: greet(req=me + span))
    pl.when(jnp.logical_not(not_last))(lambda: greet(req=me - span))

    loads = [
        pltpu.make_async_copy(source, target, local_sem.at[i])
        for i, (source, target) in enumerate(
            [(wo, wo_all.at[tp]), (cache_k, kbuf), (cache_v, vbuf), (wdown, down_v), (wup, up_v), (wk, wk_v), (wv, wv_v)]
        )
    ]
    for load in loads:
        load.start()

    normed = normalize(tokens[...].astype(F32), gain_a[...].astype(F32)[None, :])
    qbuf[me] = matmul_rows(wq[...], normed).astype(BF16)

    pl.semaphore_wait(barrier, 5)

    def whole(plane, column):
        return qbuf.at[plane * 2 + column]

    def early(plane, column):
        return qbuf.at[plane * 2 + column, pl.ds(0, FIRST)]

    def late(plane, column):
        return qbuf.at[plane * 2 + column, pl.ds(FIRST, REST)]

    def up_whole(plane):
        return remote(whole(plane, x), whole(plane, x), qsend.at[0, plane], qrecv.at[0, plane], req=me + 2)

    def up_early(plane):
        return remote(early(plane, 1 - x), early(plane, 1 - x), qsend.at[1, plane], qrecv.at[1, plane], req=me + 2)

    def down_whole(plane):
        return remote(whole(plane, x), whole(plane, x), qsend.at[2, plane], qrecv.at[0, plane], req=me - 2)

    def down_early(plane):
        return remote(early(plane, 1 - x), early(plane, 1 - x), qsend.at[3, plane], qrecv.at[1, plane], req=me - 2)

    def over_late(plane):
        return remote(late(plane, x), late(plane, x), qsend.at[4, plane], qrecv.at[2, plane], req=mate)

    over_whole = remote(whole(z, x), whole(z, x), qsend.at[4, z], qrecv.at[2, z], req=mate)
    got_whole = remote(whole(z, 1 - x), whole(z, 1 - x), qsend.at[4, z], qrecv.at[2, z], req=mate)

    over_whole.start()
    pl.when(not_last)(lambda: up_whole(z).start())
    pl.when(not_first)(lambda: down_whole(z).start())

    loads[0].wait()
    wo_y = remote(wo_all.at[tp], wo_all.at[tp], tsend.at[0], trecv.at[0], tp=y_mate)
    wo_core = remote(wo_all.at[tp], wo_all.at[tp], tsend.at[1], trecv.at[1], tp=core_mate)
    wo_y.start()
    wo_core.start()

    got_whole.wait_recv()
    pl.when(not_last)(lambda: up_early(z).start())
    pl.when(not_first)(lambda: down_early(z).start())

    loads[5].wait()
    loads[6].wait()
    own_k[...] = matmul_rows(normed, wk_v[...]).astype(BF16)
    own_v[...] = matmul_rows(wv_v[...], normed).astype(BF16)

    def save(plane, start, partial):
        for place, (numer, top, total) in enumerate(partial, start):
            numers[plane, pl.ds(place * HDIM, HDIM)] = numer
            stats[plane, pl.ds(place, 1)] = top
            stats[plane, pl.ds(8 + place, 1)] = total

    def load(plane, start, stop):
        held = stats[plane]
        return [
            (
                numers[plane, pl.ds(place * HDIM, HDIM)],
                held[place : place + 1],
                held[8 + place : 9 + place],
            )
            for place in range(start, stop)
        ]

    def cached(target):
        queries = qbuf[target]
        parts = []
        for j in range(R_DEV):
            chosen = prefix[target * R_DEV + j]
            parts.append(
                request_partial(
                    queries[:, j * SLOT : (j + 1) * SLOT], kbuf[chosen], cache_vt[chosen], False
                )
            )
        return both_requests(*parts)

    save(
        z,
        1,
        both_requests(
            *[
                request_partial(
                    qbuf[me, :, pl.ds(j * SLOT, SLOT)],
                    own_k[pl.ds(j * SLOT, SLOT), :],
                    own_v[:, pl.ds(j * SLOT, SLOT)],
                    True,
                )
                for j in range(R_DEV)
            ]
        ),
    )

    def relay(step):
        below = z - 1 - step
        above = z + 1 + step

        @pl.when(below >= 0)
        def _():
            up_whole(below).wait_recv()
            pl.when(not_last)(lambda: up_whole(below).start())
            over_late(below).start()

        @pl.when(above < nz)
        def _():
            down_whole(above).wait_recv()
            pl.when(not_first)(lambda: down_whole(above).start())
            over_late(above).start()

        @pl.when(below >= 0)
        def _():
            up_early(below).wait_recv()
            pl.when(not_last)(lambda: up_early(below).start())

        @pl.when(above < nz)
        def _():
            down_early(above).wait_recv()
            pl.when(not_first)(lambda: down_early(above).start())

    def turn(index, carry):
        cache_vt[index] = vbuf[index].T
        return carry

    relay(0)
    loads[1].wait()
    loads[2].wait()
    lax.fori_loop(0, vbuf.shape[0], turn, 0)

    def send_over(plane):
        return remote(over.at[0, plane], over.at[1, plane], osend.at[plane], orecv.at[plane], req=mate)

    def passing(buffer, kind, way, plane):
        if way == 0:
            direct = jnp.logical_and(z == 0, plane == nz - 1)
            there = me + jnp.where(direct, span, 2)
            there_slot = jnp.where(direct, nz, plane)
        else:
            direct = jnp.logical_and(z == nz - 1, plane == 0)
            there = me - jnp.where(direct, span, 2)
            there_slot = jnp.where(plane == z - 1, nz, plane)
        return remote(
            buffer.at[plane], buffer.at[there_slot], psend.at[kind, plane], precv.at[kind, there_slot], req=there
        )

    def arriving(buffer, kind, slot):
        return remote(buffer.at[slot], buffer.at[slot], psend.at[kind, slot], precv.at[kind, slot], req=mate)

    def compute(plane):
        remote(late(plane, 1 - x), late(plane, 1 - x), qsend.at[4, plane], qrecv.at[2, plane], req=mate).wait_recv()
        far = cached(plane * 2 + 1 - x)
        save(plane, 0, far[:1])
        over[0, plane] = pack_partial(far[1:])
        send_over(plane).start()
        save(plane, 1, cached(plane * 2 + x))

    def finish(way, plane, has_source):
        def pass_on(buffer, kind, partial):
            if has_source:
                arriving(buffer, kind, plane).wait_recv()
                partial = merge(partial, unpack_partial(buffer[plane]))
            buffer[plane] = pack_partial(partial)
            passing(buffer, kind, way, plane).start()

        pass_on(first_way, 0, load(plane, 0, 2))
        send_over(plane).wait_recv()
        pass_on(rest_way, 1, merge(load(plane, 2, 5), unpack_partial(over[1, plane])))

    def return_step(step, carry):
        high = z + 1 + step
        low = z - 1 - step
        starts_up = jnp.logical_or(z == 0, jnp.logical_and(z == 1, high == nz - 1))
        starts_down = jnp.logical_or(z == nz - 1, jnp.logical_and(z == nz - 2, low == 0))
        pl.when(high < nz)(lambda: compute(high))
        pl.when(jnp.logical_and(high < nz, starts_up))(lambda: finish(0, high, False))
        relay(step + 1)
        pl.when(low >= 0)(lambda: compute(low))
        pl.when(jnp.logical_and(low >= 0, starts_down))(lambda: finish(1, low, False))
        return carry

    lax.fori_loop(0, nz - 1, return_step, 0)
    def merge_step(step, carry):
        distance = nz - 3 - step
        high = z + distance
        low = z - distance
        pl.when(jnp.logical_and(high < nz, not_first))(lambda: finish(0, high, True))
        pl.when(jnp.logical_and(low >= 0, not_last))(lambda: finish(1, low, True))
        return carry

    lax.fori_loop(0, nz - 3, merge_step, 0)
    far = cached(mate)
    save(z, 0, far[:1])
    over[0, z] = pack_partial(far[1:])
    send_over(z).start()
    save(z, 1, merge(load(z, 1, 5), cached(me)))

    def gather_in(buffer, kind, slot, held):
        arriving(buffer, kind, slot).wait_recv()
        return merge(held, unpack_partial(buffer[slot]))

    firsts = load(z, 0, 2)
    firsts = gather_in(first_way, 0, z, firsts)
    firsts = gather_in(first_way, 0, nz, firsts)
    cross[0] = pack_partial(firsts[:1])
    to_mate = remote(cross.at[0], cross.at[1], xsend, xrecv, req=mate)
    to_mate.start()

    remote(wo_all.at[y_mate], wo_all.at[y_mate], tsend.at[0], trecv.at[0], tp=y_mate).wait_recv()
    wo_far = remote(wo_all.at[y_mate], wo_all.at[y_mate], tsend.at[2], trecv.at[2], tp=core_mate)
    wo_far.start()

    loads[3].wait()
    down_t[...] = down_v[...].T
    send_over(z).wait_recv()
    rest = merge(load(z, 2, 5), unpack_partial(over[1, z]))
    rest = gather_in(rest_way, 1, z, rest)
    rest = gather_in(rest_way, 1, nz, rest)
    to_mate.wait_recv()
    mine = merge(firsts[1:], unpack_partial(cross[1])) + rest
    att[tp] = jnp.concatenate([(numer / total).astype(BF16) for numer, _, total in mine], axis=0)

    att_y = remote(att.at[tp], att.at[tp], tsend.at[3], trecv.at[3], tp=y_mate)
    att_core = remote(att.at[tp], att.at[tp], tsend.at[4], trecv.at[4], tp=core_mate)
    att_y.start()
    att_core.start()

    def projected(index):
        return matmul(att[index].T, wo_all[index])

    terms = projected(tp)
    remote(wo_all.at[core_mate], wo_all.at[core_mate], tsend.at[1], trecv.at[1], tp=core_mate).wait_recv()
    remote(att.at[core_mate], att.at[core_mate], tsend.at[4], trecv.at[4], tp=core_mate).wait_recv()
    terms = terms + projected(core_mate)
    remote(att.at[y_mate], att.at[y_mate], tsend.at[3], trecv.at[3], tp=y_mate).wait_recv()
    att_far = remote(att.at[y_mate], att.at[y_mate], tsend.at[5], trecv.at[5], tp=core_mate)
    att_far.start()
    terms = terms + projected(y_mate)
    diagonal = (core_mate + 2) % 4
    remote(wo_all.at[diagonal], wo_all.at[diagonal], tsend.at[2], trecv.at[2], tp=core_mate).wait_recv()
    remote(att.at[diagonal], att.at[diagonal], tsend.at[5], trecv.at[5], tp=core_mate).wait_recv()
    terms = terms + projected(diagonal)

    middle = (tokens[...].astype(F32) + terms).astype(BF16).astype(F32)
    normed_middle = normalize(middle, gain_f[...].astype(F32)[None, :])
    loads[4].wait()
    gate = matmul_rows(up_v[...], normed_middle)
    hidden_t = (gate / (1.0 + jnp.exp(-gate))).astype(BF16)

    def down_part(index):
        return matmul(down_t[pl.ds(pl.multiple_of(index * WIDTH, 16), WIDTH)], hidden_t)

    core_out[0] = down_part(diagonal).astype(BF16)
    fold = remote(core_out.at[0], core_in.at[0], tsend.at[6], trecv.at[6], tp=core_mate)
    fold.start()
    far_part = down_part(y_mate)
    core_out[1] = down_part(core_mate).astype(BF16)
    fold_near = remote(core_out.at[1], core_in.at[1], tsend.at[8], trecv.at[8], tp=core_mate)
    fold_near.start()
    fold.wait_recv()
    y_out[...] = (far_part + core_in[0].astype(F32)).astype(BF16)
    swap = remote(y_out, y_in, tsend.at[7], trecv.at[7], tp=y_mate)
    swap.start()
    near_part = down_part(tp)
    mid_t[...] = middle.T
    near_part = near_part + mid_t[pl.ds(pl.multiple_of(tp * WIDTH, 16), WIDTH)]
    fold_near.wait_recv()
    near_part = near_part + core_in[1].astype(F32)
    lane = lax.broadcasted_iota(jnp.int32, (WIDTH, ROWS), 1)
    live = jnp.where(lane < SLOT, length[me * R_DEV], length[me * R_DEV + 1])
    swap.wait_recv()
    layer = near_part + y_in[...].astype(F32)
    out[...] = jnp.where(lane % SLOT < live, layer, 0.0).astype(BF16)

    over_whole.wait_send()

    def sent_step(plane, carry):
        pl.when(plane != z)(lambda: over_late(plane).wait_send())

        @pl.when(jnp.logical_and(not_last, plane <= z))
        def _():
            up_whole(plane).wait_send()
            up_early(plane).wait_send()

        @pl.when(jnp.logical_and(not_first, plane >= z))
        def _():
            down_whole(plane).wait_send()
            down_early(plane).wait_send()

        send_over(plane).wait_send()

        for kind, buffer in ((0, first_way), (1, rest_way)):
            pl.when(plane > z)(lambda: passing(buffer, kind, 0, plane).wait_send())
            pl.when(plane < z)(lambda: passing(buffer, kind, 1, plane).wait_send())

        return carry

    lax.fori_loop(0, nz, sent_step, 0)
    for copy in (to_mate, wo_y, wo_core, wo_far, att_y, att_core, att_far, fold, fold_near, swap):
        copy.wait_send()


def per_device(
    tokens,
    attention_gain,
    feedforward_gain,
    query_weight,
    key_weight,
    value_weight,
    out_weight,
    up_weight,
    down_weight,
    cache_keys,
    cache_values,
    request_prefix,
    suffix_length,
):
    owners = lax.axis_size("req")
    nz = owners // 2
    rows, model = tokens.shape
    prefixes = cache_keys.shape[1]
    dma = pltpu.SemaphoreType.DMA
    vmem = pl.BlockSpec(memory_space=pltpu.VMEM)
    smem = pl.BlockSpec(memory_space=pltpu.SMEM)
    away = pl.BlockSpec(memory_space=pl.ANY)
    return pl.pallas_call(
        functools.partial(kernel, nz),
        out_shape=jax.ShapeDtypeStruct((WIDTH, rows), BF16),
        in_specs=[vmem] * 4 + [away] * 7 + [smem] * 2,
        out_specs=vmem,
        scratch_shapes=[
            pltpu.VMEM((owners, WIDTH, ROWS), BF16),
            pltpu.VMEM((prefixes, PG, WIDTH), BF16),
            pltpu.VMEM((prefixes, PG, WIDTH), BF16),
            pltpu.VMEM((4, WIDTH, model), BF16),
            pltpu.VMEM((WIDTH, model), BF16),
            pltpu.VMEM((WIDTH, model), BF16),
            pltpu.VMEM((model, WIDTH), BF16),
            pltpu.VMEM((ROWS, WIDTH), BF16),
            pltpu.VMEM((WIDTH, ROWS), BF16),
            pltpu.VMEM((prefixes, WIDTH, PG), BF16),
            pltpu.VMEM((nz, FIRST + WIDTH, ROWS), F32),
            pltpu.VMEM((nz, STATS, ROWS), F32),
            pltpu.VMEM((nz + 1, REST + STATS, ROWS), BF16),
            pltpu.VMEM((nz + 1, 2 * FIRST + STATS, ROWS), BF16),
            pltpu.VMEM((2, nz, REST + STATS, ROWS), BF16),
            pltpu.VMEM((2, FIRST + STATS, ROWS), BF16),
            pltpu.VMEM((4, WIDTH, ROWS), BF16),
            pltpu.VMEM((2, WIDTH, ROWS), BF16),
            pltpu.VMEM((2, WIDTH, ROWS), BF16),
            pltpu.VMEM((WIDTH, ROWS), BF16),
            pltpu.VMEM((WIDTH, ROWS), BF16),
            pltpu.VMEM((model, ROWS), F32),
            dma((7,)),
            dma((5, nz)),
            dma((3, nz)),
            dma((2, nz + 1)),
            dma((2, nz + 1)),
            dma,
            dma,
            dma((9,)),
            dma((9,)),
            dma((nz,)),
            dma((nz,)),
            pltpu.VMEM((WIDTH, model), BF16),
            pltpu.VMEM((WIDTH, model), BF16),
        ],
        compiler_params=pltpu.CompilerParams(
            collective_id=0, has_side_effects=True, vmem_limit_bytes=60 * 1024 * 1024
        ),
    )(
        tokens,
        attention_gain,
        feedforward_gain,
        query_weight.T,
        key_weight.T,
        value_weight.T,
        out_weight,
        up_weight.T,
        down_weight,
        cache_keys[0],
        cache_values[0],
        request_prefix,
        suffix_length,
    ).T


def solution(mesh):
    in_specs = (
        P("req", None),
        P(),
        P(),
        P(None, "tp"),
        P(None, "tp"),
        P(None, "tp"),
        P("tp", None),
        P(None, "tp"),
        P("tp", None),
        P("req", None, None, "tp"),
        P("req", None, None, "tp"),
        P(),
        P(),
    )
    out_specs = P("req", "tp")
    return jax.shard_map(
        per_device, mesh=mesh, in_specs=in_specs, out_specs=out_specs, check_vma=False
    )
```

```python
import functools
import math

import jax
import jax.numpy as jnp
from jax import lax
from jax.experimental import pallas as pl
from jax.experimental.pallas import tpu as pltpu
from jax.sharding import PartitionSpec as P

HDIM = 80
SLOT = 128
R_DEV = 2
PG = 192
LOCAL_HEADS = 4
WIDTH = HDIM * LOCAL_HEADS
ROWS = R_DEV * SLOT
STATS = 16
FIRST = HDIM
REST = WIDTH - HDIM

EPSILON = 1e-06
NEGATIVE = -1e30
MESH = pl.DeviceIdType.MESH
F32 = jnp.float32
BF16 = jnp.bfloat16


def normalize(floats, gain):
    mean_square = jnp.mean(floats * floats, axis=-1, keepdims=True)
    return (floats * lax.rsqrt(mean_square + EPSILON) * gain).astype(BF16)


def matmul(left, right):
    return jnp.dot(left, right, preferred_element_type=F32)


def matmul_rows(left, right):
    return lax.dot_general(left, right, (((1,), (1,)), ((), ())), preferred_element_type=F32)


def head_rows(values, head):
    return values[head * HDIM : (head + 1) * HDIM]


def request_partial(query_t, keys, values_t, causal):
    none = jnp.zeros((HDIM, SLOT), BF16)
    partial = []
    for pair, (start, stop) in enumerate(((0, 256), (128, WIDTH))):
        first, second = head_rows(query_t, 2 * pair), head_rows(query_t, 2 * pair + 1)
        above = 2 * pair * HDIM - start
        below = stop - start - above - 2 * HDIM
        blocks = [jnp.zeros((above, 2 * SLOT), BF16)] if above else []
        blocks.append(jnp.concatenate([first, none], axis=1))
        blocks.append(jnp.concatenate([none, second], axis=1))
        if below:
            blocks.append(jnp.zeros((below, 2 * SLOT), BF16))
        scores = matmul(keys[:, start:stop], jnp.concatenate(blocks, axis=0)) * (1.0 / math.sqrt(HDIM))
        if causal:
            key_row = lax.broadcasted_iota(jnp.int32, scores.shape, 0)
            query_row = lax.broadcasted_iota(jnp.int32, scores.shape, 1) % SLOT
            scores = jnp.where(key_row <= query_row, scores, NEGATIVE)
        top = jnp.max(scores, axis=0, keepdims=True)
        if not causal:
            top = top.astype(BF16).astype(F32)
        weights = jnp.exp(scores - top)
        total = jnp.sum(weights, axis=0, keepdims=True)
        numer = matmul(values_t[2 * pair * HDIM : 2 * (pair + 1) * HDIM], weights.astype(BF16))
        partial.append((numer[:HDIM, :SLOT], top[:, :SLOT], total[:, :SLOT]))
        partial.append((numer[HDIM:, SLOT:], top[:, SLOT:], total[:, SLOT:]))
    return partial


def both_requests(first, second):
    return [
        tuple(jnp.concatenate([a, b], axis=1) for a, b in zip(first[h], second[h]))
        for h in range(LOCAL_HEADS)
    ]


def merge(one, other):
    merged = []
    for (numer_a, top_a, total_a), (numer_b, top_b, total_b) in zip(one, other):
        top = jnp.maximum(top_a, top_b)
        factor_a = jnp.exp(top_a - top)
        factor_b = jnp.exp(top_b - top)
        merged.append(
            (
                numer_a * factor_a + numer_b * factor_b,
                top,
                total_a * factor_a + total_b * factor_b,
            )
        )
    return merged


def pack_partial(partial):
    heads = len(partial)
    shares = [(numer / total).astype(BF16) for numer, _, total in partial]
    tops = [top for _, top, _ in partial]
    whole = [total.astype(BF16).astype(F32) for _, _, total in partial]
    rest = [total - high for (_, _, total), high in zip(partial, whole)]
    pad = [jnp.zeros((STATS - 3 * heads, ROWS), F32)]
    stats = jnp.concatenate(tops + whole + rest + pad, axis=0).astype(BF16)
    return jnp.concatenate(shares + [stats], axis=0)


def unpack_partial(block):
    heads = (block.shape[0] - STATS) // HDIM
    stats = block[heads * HDIM :].astype(F32)
    partial = []
    for h in range(heads):
        top = stats[h : h + 1]
        total = stats[heads + h : heads + h + 1]
        total = total + stats[2 * heads + h : 2 * heads + h + 1]
        partial.append((head_rows(block, h).astype(F32) * total, top, total))
    return partial


def kernel(
    nz,
    tokens,
    gain_a,
    gain_f,
    wq,
    wk,
    wv,
    wo,
    wup,
    wdown,
    cache_k,
    cache_v,
    prefix,
    length,
    out,
    qbuf,
    kbuf,
    vbuf,
    wo_all,
    up_v,
    down_v,
    down_t,
    own_k,
    own_v,
    cache_vt,
    numers,
    stats,
    rest_way,
    first_way,
    over,
    cross,
    att,
    core_out,
    core_in,
    y_out,
    y_in,
    mid_t,
    local_sem,
    qsend,
    qrecv,
    psend,
    precv,
    xsend,
    xrecv,
    tsend,
    trecv,
    osend,
    orecv,
    wk_v,
    wv_v,
):
    me = lax.axis_index("req")
    tp = lax.axis_index("tp")
    z = me // 2
    x = me % 2
    mate = z * 2 + 1 - x
    core_mate = tp + 1 - 2 * (tp % 2)
    y_mate = (tp + 2) % 4
    not_first = z > 0
    not_last = z < nz - 1

    def remote(source, target, send_sem, recv_sem, **where):
        return pltpu.make_async_remote_copy(
            src_ref=source,
            dst_ref=target,
            send_sem=send_sem,
            recv_sem=recv_sem,
            device_id=where,
            device_id_type=MESH,
        )

    barrier = pltpu.get_barrier_semaphore()

    def greet(**where):
        pl.semaphore_signal(barrier, inc=1, device_id=where, device_id_type=MESH)

    greet(req=mate)
    greet(tp=core_mate)
    greet(tp=y_mate)
    pl.when(not_first)(lambda: greet(req=me - 2))
    pl.when(not_last)(lambda: greet(req=me + 2))
    span = 2 * (nz - 1)
    pl.when(jnp.logical_not(not_first))(lambda: greet(req=me + span))
    pl.when(jnp.logical_not(not_last))(lambda: greet(req=me - span))

    loads = [
        pltpu.make_async_copy(source, target, local_sem.at[i])
        for i, (source, target) in enumerate(
            [(wo, wo_all.at[tp]), (cache_k, kbuf), (cache_v, vbuf), (wdown, down_v), (wup, up_v), (wk, wk_v), (wv, wv_v)]
        )
    ]
    for load in loads:
        load.start()

    normed = normalize(tokens[...].astype(F32), gain_a[...].astype(F32)[None, :])
    qbuf[me] = matmul_rows(wq[...], normed).astype(BF16)

    pl.semaphore_wait(barrier, 5)

    def whole(plane, column):
        return qbuf.at[plane * 2 + column]

    def early(plane, column):
        return qbuf.at[plane * 2 + column, pl.ds(0, FIRST)]

    def late(plane, column):
        return qbuf.at[plane * 2 + column, pl.ds(FIRST, REST)]

    def up_whole(plane):
        return remote(whole(plane, x), whole(plane, x), qsend.at[0, plane], qrecv.at[0, plane], req=me + 2)

    def up_early(plane):
        return remote(early(plane, 1 - x), early(plane, 1 - x), qsend.at[1, plane], qrecv.at[1, plane], req=me + 2)

    def down_whole(plane):
        return remote(whole(plane, x), whole(plane, x), qsend.at[2, plane], qrecv.at[0, plane], req=me - 2)

    def down_early(plane):
        return remote(early(plane, 1 - x), early(plane, 1 - x), qsend.at[3, plane], qrecv.at[1, plane], req=me - 2)

    def over_late(plane):
        return remote(late(plane, x), late(plane, x), qsend.at[4, plane], qrecv.at[2, plane], req=mate)

    over_whole = remote(whole(z, x), whole(z, x), qsend.at[4, z], qrecv.at[2, z], req=mate)
    got_whole = remote(whole(z, 1 - x), whole(z, 1 - x), qsend.at[4, z], qrecv.at[2, z], req=mate)

    over_whole.start()
    pl.when(not_last)(lambda: up_whole(z).start())
    pl.when(not_first)(lambda: down_whole(z).start())

    got_whole.wait_recv()
    pl.when(not_last)(lambda: up_early(z).start())
    pl.when(not_first)(lambda: down_early(z).start())

    def save(plane, start, partial):
        for place, (numer, top, total) in enumerate(partial, start):
            numers[plane, pl.ds(place * HDIM, HDIM)] = numer
            stats[plane, pl.ds(place, 1)] = top
            stats[plane, pl.ds(8 + place, 1)] = total

    def load(plane, start, stop):
        held = stats[plane]
        return [
            (
                numers[plane, pl.ds(place * HDIM, HDIM)],
                held[place : place + 1],
                held[8 + place : 9 + place],
            )
            for place in range(start, stop)
        ]

    def cached(target):
        queries = qbuf[target]
        parts = []
        for j in range(R_DEV):
            chosen = prefix[target * R_DEV + j]
            parts.append(
                request_partial(
                    queries[:, j * SLOT : (j + 1) * SLOT], kbuf[chosen], cache_vt[chosen], False
                )
            )
        return both_requests(*parts)

    def relay(step):
        below = z - 1 - step
        above = z + 1 + step

        @pl.when(below >= 0)
        def _():
            up_whole(below).wait_recv()
            pl.when(not_last)(lambda: up_whole(below).start())
            over_late(below).start()

        @pl.when(above < nz)
        def _():
            down_whole(above).wait_recv()
            pl.when(not_first)(lambda: down_whole(above).start())
            over_late(above).start()

        @pl.when(below >= 0)
        def _():
            up_early(below).wait_recv()
            pl.when(not_last)(lambda: up_early(below).start())

        @pl.when(above < nz)
        def _():
            down_early(above).wait_recv()
            pl.when(not_first)(lambda: down_early(above).start())

    def turn(index, carry):
        cache_vt[index] = vbuf[index].T
        return carry

    loads[2].wait()
    lax.fori_loop(0, vbuf.shape[0], turn, 0)

    loads[0].wait()
    wo_y = remote(wo_all.at[tp], wo_all.at[tp], tsend.at[0], trecv.at[0], tp=y_mate)
    wo_core = remote(wo_all.at[tp], wo_all.at[tp], tsend.at[1], trecv.at[1], tp=core_mate)
    wo_y.start()
    wo_core.start()
    loads[1].wait()
    relay(0)
    def send_over(plane):
        return remote(over.at[0, plane], over.at[1, plane], osend.at[plane], orecv.at[plane], req=mate)

    def passing(buffer, kind, way, plane):
        if way == 0:
            direct = jnp.logical_and(z == 0, plane == nz - 1)
            there = me + jnp.where(direct, span, 2)
            there_slot = jnp.where(direct, nz, plane)
        else:
            direct = jnp.logical_and(z == nz - 1, plane == 0)
            there = me - jnp.where(direct, span, 2)
            there_slot = jnp.where(plane == z - 1, nz, plane)
        return remote(
            buffer.at[plane], buffer.at[there_slot], psend.at[kind, plane], precv.at[kind, there_slot], req=there
        )

    def arriving(buffer, kind, slot):
        return remote(buffer.at[slot], buffer.at[slot], psend.at[kind, slot], precv.at[kind, slot], req=mate)

    def compute(plane):
        remote(late(plane, 1 - x), late(plane, 1 - x), qsend.at[4, plane], qrecv.at[2, plane], req=mate).wait_recv()
        far = cached(plane * 2 + 1 - x)
        save(plane, 0, far[:1])
        over[0, plane] = pack_partial(far[1:])
        send_over(plane).start()
        save(plane, 1, cached(plane * 2 + x))

    def finish(way, plane, has_source):
        def pass_on(buffer, kind, partial):
            if has_source:
                arriving(buffer, kind, plane).wait_recv()
                partial = merge(partial, unpack_partial(buffer[plane]))
            buffer[plane] = pack_partial(partial)
            passing(buffer, kind, way, plane).start()

        pass_on(first_way, 0, load(plane, 0, 2))
        send_over(plane).wait_recv()
        pass_on(rest_way, 1, merge(load(plane, 2, 5), unpack_partial(over[1, plane])))

    def return_step(step, carry):
        high = z + 1 + step
        low = z - 1 - step
        starts_up = jnp.logical_or(z == 0, jnp.logical_and(z == 1, high == nz - 1))
        starts_down = jnp.logical_or(z == nz - 1, jnp.logical_and(z == nz - 2, low == 0))
        pl.when(high < nz)(lambda: compute(high))
        pl.when(jnp.logical_and(high < nz, starts_up))(lambda: finish(0, high, False))
        relay(step + 1)
        pl.when(low >= 0)(lambda: compute(low))
        pl.when(jnp.logical_and(low >= 0, starts_down))(lambda: finish(1, low, False))
        return carry

    lax.fori_loop(0, nz - 1, return_step, 0)
    def merge_step(step, carry):
        distance = nz - 3 - step
        high = z + distance
        low = z - distance
        pl.when(jnp.logical_and(high < nz, not_first))(lambda: finish(0, high, True))
        pl.when(jnp.logical_and(low >= 0, not_last))(lambda: finish(1, low, True))
        return carry

    lax.fori_loop(0, nz - 3, merge_step, 0)
    far = cached(mate)
    save(z, 0, far[:1])
    over[0, z] = pack_partial(far[1:])
    send_over(z).start()
    loads[5].wait()
    loads[6].wait()
    own_k[...] = matmul_rows(normed, wk_v[...]).astype(BF16)
    own_v[...] = matmul_rows(wv_v[...], normed).astype(BF16)
    save(
        z,
        1,
        both_requests(
            *[
                request_partial(
                    qbuf[me, :, pl.ds(j * SLOT, SLOT)],
                    own_k[pl.ds(j * SLOT, SLOT), :],
                    own_v[:, pl.ds(j * SLOT, SLOT)],
                    True,
                )
                for j in range(R_DEV)
            ]
        ),
    )
    save(z, 1, merge(load(z, 1, 5), cached(me)))

    def gather_in(buffer, kind, slot, held):
        arriving(buffer, kind, slot).wait_recv()
        return merge(held, unpack_partial(buffer[slot]))

    firsts = load(z, 0, 2)
    firsts = gather_in(first_way, 0, z, firsts)
    firsts = gather_in(first_way, 0, nz, firsts)
    cross[0] = pack_partial(firsts[:1])
    to_mate = remote(cross.at[0], cross.at[1], xsend, xrecv, req=mate)
    to_mate.start()

    remote(wo_all.at[y_mate], wo_all.at[y_mate], tsend.at[0], trecv.at[0], tp=y_mate).wait_recv()
    wo_far = remote(wo_all.at[y_mate], wo_all.at[y_mate], tsend.at[2], trecv.at[2], tp=core_mate)
    wo_far.start()

    loads[3].wait()
    down_t[...] = down_v[...].T
    send_over(z).wait_recv()
    rest = merge(load(z, 2, 5), unpack_partial(over[1, z]))
    rest = gather_in(rest_way, 1, z, rest)
    rest = gather_in(rest_way, 1, nz, rest)
    to_mate.wait_recv()
    mine = merge(firsts[1:], unpack_partial(cross[1])) + rest
    att[tp] = jnp.concatenate([(numer / total).astype(BF16) for numer, _, total in mine], axis=0)

    att_y = remote(att.at[tp], att.at[tp], tsend.at[3], trecv.at[3], tp=y_mate)
    att_core = remote(att.at[tp], att.at[tp], tsend.at[4], trecv.at[4], tp=core_mate)
    att_y.start()
    att_core.start()

    def projected(index):
        return matmul(att[index].T, wo_all[index])

    terms = projected(tp)
    remote(wo_all.at[core_mate], wo_all.at[core_mate], tsend.at[1], trecv.at[1], tp=core_mate).wait_recv()
    remote(att.at[core_mate], att.at[core_mate], tsend.at[4], trecv.at[4], tp=core_mate).wait_recv()
    terms = terms + projected(core_mate)
    remote(att.at[y_mate], att.at[y_mate], tsend.at[3], trecv.at[3], tp=y_mate).wait_recv()
    att_far = remote(att.at[y_mate], att.at[y_mate], tsend.at[5], trecv.at[5], tp=core_mate)
    att_far.start()
    terms = terms + projected(y_mate)
    diagonal = (core_mate + 2) % 4
    remote(wo_all.at[diagonal], wo_all.at[diagonal], tsend.at[2], trecv.at[2], tp=core_mate).wait_recv()
    remote(att.at[diagonal], att.at[diagonal], tsend.at[5], trecv.at[5], tp=core_mate).wait_recv()
    terms = terms + projected(diagonal)

    middle = (tokens[...].astype(F32) + terms).astype(BF16).astype(F32)
    normed_middle = normalize(middle, gain_f[...].astype(F32)[None, :])
    loads[4].wait()
    gate = matmul_rows(up_v[...], normed_middle)
    hidden_t = (gate / (1.0 + jnp.exp(-gate))).astype(BF16)

    def down_part(index):
        return matmul(down_t[pl.ds(pl.multiple_of(index * WIDTH, 16), WIDTH)], hidden_t)

    core_out[0] = down_part(diagonal).astype(BF16)
    fold = remote(core_out.at[0], core_in.at[0], tsend.at[6], trecv.at[6], tp=core_mate)
    fold.start()
    far_part = down_part(y_mate)
    core_out[1] = down_part(core_mate).astype(BF16)
    fold_near = remote(core_out.at[1], core_in.at[1], tsend.at[8], trecv.at[8], tp=core_mate)
    fold_near.start()
    fold.wait_recv()
    y_out[...] = (far_part + core_in[0].astype(F32)).astype(BF16)
    swap = remote(y_out, y_in, tsend.at[7], trecv.at[7], tp=y_mate)
    swap.start()
    near_part = down_part(tp)
    mid_t[...] = middle.T
    near_part = near_part + mid_t[pl.ds(pl.multiple_of(tp * WIDTH, 16), WIDTH)]
    fold_near.wait_recv()
    near_part = near_part + core_in[1].astype(F32)
    lane = lax.broadcasted_iota(jnp.int32, (WIDTH, ROWS), 1)
    live = jnp.where(lane < SLOT, length[me * R_DEV], length[me * R_DEV + 1])
    swap.wait_recv()
    layer = near_part + y_in[...].astype(F32)
    out[...] = jnp.where(lane % SLOT < live, layer, 0.0).astype(BF16)

    over_whole.wait_send()

    def sent_step(plane, carry):
        pl.when(plane != z)(lambda: over_late(plane).wait_send())

        @pl.when(jnp.logical_and(not_last, plane <= z))
        def _():
            up_whole(plane).wait_send()
            up_early(plane).wait_send()

        @pl.when(jnp.logical_and(not_first, plane >= z))
        def _():
            down_whole(plane).wait_send()
            down_early(plane).wait_send()

        send_over(plane).wait_send()

        for kind, buffer in ((0, first_way), (1, rest_way)):
            pl.when(plane > z)(lambda: passing(buffer, kind, 0, plane).wait_send())
            pl.when(plane < z)(lambda: passing(buffer, kind, 1, plane).wait_send())

        return carry

    lax.fori_loop(0, nz, sent_step, 0)
    for copy in (to_mate, wo_y, wo_core, wo_far, att_y, att_core, att_far, fold, fold_near, swap):
        copy.wait_send()


def per_device(
    tokens,
    attention_gain,
    feedforward_gain,
    query_weight,
    key_weight,
    value_weight,
    out_weight,
    up_weight,
    down_weight,
    cache_keys,
    cache_values,
    request_prefix,
    suffix_length,
):
    owners = lax.axis_size("req")
    nz = owners // 2
    rows, model = tokens.shape
    prefixes = cache_keys.shape[1]
    dma = pltpu.SemaphoreType.DMA
    vmem = pl.BlockSpec(memory_space=pltpu.VMEM)
    smem = pl.BlockSpec(memory_space=pltpu.SMEM)
    away = pl.BlockSpec(memory_space=pl.ANY)
    return pl.pallas_call(
        functools.partial(kernel, nz),
        out_shape=jax.ShapeDtypeStruct((WIDTH, rows), BF16),
        in_specs=[vmem] * 4 + [away] * 7 + [smem] * 2,
        out_specs=vmem,
        scratch_shapes=[
            pltpu.VMEM((owners, WIDTH, ROWS), BF16),
            pltpu.VMEM((prefixes, PG, WIDTH), BF16),
            pltpu.VMEM((prefixes, PG, WIDTH), BF16),
            pltpu.VMEM((4, WIDTH, model), BF16),
            pltpu.VMEM((WIDTH, model), BF16),
            pltpu.VMEM((WIDTH, model), BF16),
            pltpu.VMEM((model, WIDTH), BF16),
            pltpu.VMEM((ROWS, WIDTH), BF16),
            pltpu.VMEM((WIDTH, ROWS), BF16),
            pltpu.VMEM((prefixes, WIDTH, PG), BF16),
            pltpu.VMEM((nz, FIRST + WIDTH, ROWS), F32),
            pltpu.VMEM((nz, STATS, ROWS), F32),
            pltpu.VMEM((nz + 1, REST + STATS, ROWS), BF16),
            pltpu.VMEM((nz + 1, 2 * FIRST + STATS, ROWS), BF16),
            pltpu.VMEM((2, nz, REST + STATS, ROWS), BF16),
            pltpu.VMEM((2, FIRST + STATS, ROWS), BF16),
            pltpu.VMEM((4, WIDTH, ROWS), BF16),
            pltpu.VMEM((2, WIDTH, ROWS), BF16),
            pltpu.VMEM((2, WIDTH, ROWS), BF16),
            pltpu.VMEM((WIDTH, ROWS), BF16),
            pltpu.VMEM((WIDTH, ROWS), BF16),
            pltpu.VMEM((model, ROWS), F32),
            dma((7,)),
            dma((5, nz)),
            dma((3, nz)),
            dma((2, nz + 1)),
            dma((2, nz + 1)),
            dma,
            dma,
            dma((9,)),
            dma((9,)),
            dma((nz,)),
            dma((nz,)),
            pltpu.VMEM((WIDTH, model), BF16),
            pltpu.VMEM((WIDTH, model), BF16),
        ],
        compiler_params=pltpu.CompilerParams(
            collective_id=0, has_side_effects=True, vmem_limit_bytes=60 * 1024 * 1024
        ),
    )(
        tokens,
        attention_gain,
        feedforward_gain,
        query_weight.T,
        key_weight.T,
        value_weight.T,
        out_weight,
        up_weight.T,
        down_weight,
        cache_keys[0],
        cache_values[0],
        request_prefix,
        suffix_length,
    ).T


def solution(mesh):
    in_specs = (
        P("req", None),
        P(),
        P(),
        P(None, "tp"),
        P(None, "tp"),
        P(None, "tp"),
        P("tp", None),
        P(None, "tp"),
        P("tp", None),
        P("req", None, None, "tp"),
        P("req", None, None, "tp"),
        P(),
        P(),
    )
    out_specs = P("req", "tp")
    return jax.shard_map(
        per_device, mesh=mesh, in_specs=in_specs, out_specs=out_specs, check_vma=False
    )
```

```python
import functools
import math

import jax
import jax.numpy as jnp
from jax import lax
from jax.experimental import pallas as pl
from jax.experimental.pallas import tpu as pltpu
from jax.sharding import PartitionSpec as P

HDIM = 80
SLOT = 128
R_DEV = 2
PG = 192
LOCAL_HEADS = 4
WIDTH = HDIM * LOCAL_HEADS
ROWS = R_DEV * SLOT
STATS = 16
FIRST = HDIM
REST = WIDTH - HDIM

EPSILON = 1e-06
NEGATIVE = -1e30
MESH = pl.DeviceIdType.MESH
F32 = jnp.float32
BF16 = jnp.bfloat16


def normalize(floats, gain):
    mean_square = jnp.mean(floats * floats, axis=-1, keepdims=True)
    return (floats * lax.rsqrt(mean_square + EPSILON) * gain).astype(BF16)


def matmul(left, right):
    return jnp.dot(left, right, preferred_element_type=F32)


def matmul_rows(left, right):
    return lax.dot_general(left, right, (((1,), (1,)), ((), ())), preferred_element_type=F32)


def head_rows(values, head):
    return values[head * HDIM : (head + 1) * HDIM]


def request_partial(query_t, keys, values_t, causal):
    none = jnp.zeros((HDIM, SLOT), BF16)
    partial = []
    for pair, (start, stop) in enumerate(((0, 256), (128, WIDTH))):
        first, second = head_rows(query_t, 2 * pair), head_rows(query_t, 2 * pair + 1)
        above = 2 * pair * HDIM - start
        below = stop - start - above - 2 * HDIM
        blocks = [jnp.zeros((above, 2 * SLOT), BF16)] if above else []
        blocks.append(jnp.concatenate([first, none], axis=1))
        blocks.append(jnp.concatenate([none, second], axis=1))
        if below:
            blocks.append(jnp.zeros((below, 2 * SLOT), BF16))
        scores = matmul(keys[:, start:stop], jnp.concatenate(blocks, axis=0)) * (1.0 / math.sqrt(HDIM))
        if causal:
            key_row = lax.broadcasted_iota(jnp.int32, scores.shape, 0)
            query_row = lax.broadcasted_iota(jnp.int32, scores.shape, 1) % SLOT
            scores = jnp.where(key_row <= query_row, scores, NEGATIVE)
        top = jnp.max(scores, axis=0, keepdims=True)
        if not causal:
            top = top.astype(BF16).astype(F32)
        weights = jnp.exp(scores - top)
        total = jnp.sum(weights, axis=0, keepdims=True)
        numer = matmul(values_t[2 * pair * HDIM : 2 * (pair + 1) * HDIM], weights.astype(BF16))
        partial.append((numer[:HDIM, :SLOT], top[:, :SLOT], total[:, :SLOT]))
        partial.append((numer[HDIM:, SLOT:], top[:, SLOT:], total[:, SLOT:]))
    return partial


def both_requests(first, second):
    return [
        tuple(jnp.concatenate([a, b], axis=1) for a, b in zip(first[h], second[h]))
        for h in range(LOCAL_HEADS)
    ]


def merge(one, other):
    merged = []
    for (numer_a, top_a, total_a), (numer_b, top_b, total_b) in zip(one, other):
        top = jnp.maximum(top_a, top_b)
        factor_a = jnp.exp(top_a - top)
        factor_b = jnp.exp(top_b - top)
        merged.append(
            (
                numer_a * factor_a + numer_b * factor_b,
                top,
                total_a * factor_a + total_b * factor_b,
            )
        )
    return merged


def pack_partial(partial):
    heads = len(partial)
    shares = [(numer / total).astype(BF16) for numer, _, total in partial]
    tops = [top for _, top, _ in partial]
    whole = [total.astype(BF16).astype(F32) for _, _, total in partial]
    rest = [total - high for (_, _, total), high in zip(partial, whole)]
    pad = [jnp.zeros((STATS - 3 * heads, ROWS), F32)]
    stats = jnp.concatenate(tops + whole + rest + pad, axis=0).astype(BF16)
    return jnp.concatenate(shares + [stats], axis=0)


def unpack_partial(block):
    heads = (block.shape[0] - STATS) // HDIM
    stats = block[heads * HDIM :].astype(F32)
    partial = []
    for h in range(heads):
        top = stats[h : h + 1]
        total = stats[heads + h : heads + h + 1]
        total = total + stats[2 * heads + h : 2 * heads + h + 1]
        partial.append((head_rows(block, h).astype(F32) * total, top, total))
    return partial


def kernel(
    nz,
    tokens,
    gain_a,
    gain_f,
    wq,
    wk,
    wv,
    wo,
    wup,
    wdown,
    cache_k,
    cache_v,
    prefix,
    length,
    out,
    qbuf,
    kbuf,
    vbuf,
    wo_all,
    up_v,
    down_v,
    down_t,
    own_k,
    own_v,
    cache_vt,
    numers,
    stats,
    rest_way,
    first_way,
    over,
    cross,
    att,
    core_out,
    core_in,
    y_out,
    y_in,
    mid_t,
    local_sem,
    qsend,
    qrecv,
    psend,
    precv,
    xsend,
    xrecv,
    tsend,
    trecv,
    osend,
    orecv,
    wk_v,
    wv_v,
):
    me = lax.axis_index("req")
    tp = lax.axis_index("tp")
    z = me // 2
    x = me % 2
    mate = z * 2 + 1 - x
    core_mate = tp + 1 - 2 * (tp % 2)
    y_mate = (tp + 2) % 4
    not_first = z > 0
    not_last = z < nz - 1

    def remote(source, target, send_sem, recv_sem, **where):
        return pltpu.make_async_remote_copy(
            src_ref=source,
            dst_ref=target,
            send_sem=send_sem,
            recv_sem=recv_sem,
            device_id=where,
            device_id_type=MESH,
        )

    barrier = pltpu.get_barrier_semaphore()

    def greet(**where):
        pl.semaphore_signal(barrier, inc=1, device_id=where, device_id_type=MESH)

    greet(req=mate)
    greet(tp=core_mate)
    greet(tp=y_mate)
    pl.when(not_first)(lambda: greet(req=me - 2))
    pl.when(not_last)(lambda: greet(req=me + 2))
    span = 2 * (nz - 1)
    pl.when(jnp.logical_not(not_first))(lambda: greet(req=me + span))
    pl.when(jnp.logical_not(not_last))(lambda: greet(req=me - span))

    loads = [
        pltpu.make_async_copy(source, target, local_sem.at[i])
        for i, (source, target) in enumerate(
            [(wo, wo_all.at[tp]), (cache_k, kbuf), (cache_v, vbuf), (wdown, down_v), (wup, up_v), (wk, wk_v), (wv, wv_v)]
        )
    ]
    for load in loads:
        load.start()

    normed = normalize(tokens[...].astype(F32), gain_a[...].astype(F32)[None, :])
    qbuf[me] = matmul_rows(wq[...], normed).astype(BF16)

    pl.semaphore_wait(barrier, 5)

    def whole(plane, column):
        return qbuf.at[plane * 2 + column]

    def early(plane, column):
        return qbuf.at[plane * 2 + column, pl.ds(0, FIRST)]

    def late(plane, column):
        return qbuf.at[plane * 2 + column, pl.ds(FIRST, REST)]

    def up_whole(plane):
        return remote(whole(plane, x), whole(plane, x), qsend.at[0, plane], qrecv.at[0, plane], req=me + 2)

    def up_early(plane):
        return remote(early(plane, 1 - x), early(plane, 1 - x), qsend.at[1, plane], qrecv.at[1, plane], req=me + 2)

    def down_whole(plane):
        return remote(whole(plane, x), whole(plane, x), qsend.at[2, plane], qrecv.at[0, plane], req=me - 2)

    def down_early(plane):
        return remote(early(plane, 1 - x), early(plane, 1 - x), qsend.at[3, plane], qrecv.at[1, plane], req=me - 2)

    def over_late(plane):
        return remote(late(plane, x), late(plane, x), qsend.at[4, plane], qrecv.at[2, plane], req=mate)

    over_whole = remote(whole(z, x), whole(z, x), qsend.at[4, z], qrecv.at[2, z], req=mate)
    got_whole = remote(whole(z, 1 - x), whole(z, 1 - x), qsend.at[4, z], qrecv.at[2, z], req=mate)

    over_whole.start()
    pl.when(not_last)(lambda: up_whole(z).start())
    pl.when(not_first)(lambda: down_whole(z).start())

    got_whole.wait_recv()
    pl.when(not_last)(lambda: up_early(z).start())
    pl.when(not_first)(lambda: down_early(z).start())

    loads[5].wait()
    loads[6].wait()
    own_k[...] = matmul_rows(normed, wk_v[...]).astype(BF16)
    own_v[...] = matmul_rows(wv_v[...], normed).astype(BF16)

    def save(plane, start, partial):
        for place, (numer, top, total) in enumerate(partial, start):
            numers[plane, pl.ds(place * HDIM, HDIM)] = numer
            stats[plane, pl.ds(place, 1)] = top
            stats[plane, pl.ds(8 + place, 1)] = total

    def load(plane, start, stop):
        held = stats[plane]
        return [
            (
                numers[plane, pl.ds(place * HDIM, HDIM)],
                held[place : place + 1],
                held[8 + place : 9 + place],
            )
            for place in range(start, stop)
        ]

    def cached(target):
        queries = qbuf[target]
        parts = []
        for j in range(R_DEV):
            chosen = prefix[target * R_DEV + j]
            parts.append(
                request_partial(
                    queries[:, j * SLOT : (j + 1) * SLOT], kbuf[chosen], cache_vt[chosen], False
                )
            )
        return both_requests(*parts)

    save(
        z,
        1,
        both_requests(
            *[
                request_partial(
                    qbuf[me, :, pl.ds(j * SLOT, SLOT)],
                    own_k[pl.ds(j * SLOT, SLOT), :],
                    own_v[:, pl.ds(j * SLOT, SLOT)],
                    True,
                )
                for j in range(R_DEV)
            ]
        ),
    )

    def relay(step):
        below = z - 1 - step
        above = z + 1 + step

        @pl.when(below >= 0)
        def _():
            up_whole(below).wait_recv()
            pl.when(not_last)(lambda: up_whole(below).start())
            over_late(below).start()

        @pl.when(above < nz)
        def _():
            down_whole(above).wait_recv()
            pl.when(not_first)(lambda: down_whole(above).start())
            over_late(above).start()

        @pl.when(below >= 0)
        def _():
            up_early(below).wait_recv()
            pl.when(not_last)(lambda: up_early(below).start())

        @pl.when(above < nz)
        def _():
            down_early(above).wait_recv()
            pl.when(not_first)(lambda: down_early(above).start())

    def turn(index, carry):
        cache_vt[index] = vbuf[index].T
        return carry

    relay(0)
    loads[1].wait()
    loads[2].wait()
    lax.fori_loop(0, vbuf.shape[0], turn, 0)

    def send_over(plane):
        return remote(over.at[0, plane], over.at[1, plane], osend.at[plane], orecv.at[plane], req=mate)

    def passing(buffer, kind, way, plane):
        if way == 0:
            direct = jnp.logical_and(z == 0, plane == nz - 1)
            there = me + jnp.where(direct, span, 2)
            there_slot = jnp.where(direct, nz, plane)
        else:
            direct = jnp.logical_and(z == nz - 1, plane == 0)
            there = me - jnp.where(direct, span, 2)
            there_slot = jnp.where(plane == z - 1, nz, plane)
        return remote(
            buffer.at[plane], buffer.at[there_slot], psend.at[kind, plane], precv.at[kind, there_slot], req=there
        )

    def arriving(buffer, kind, slot):
        return remote(buffer.at[slot], buffer.at[slot], psend.at[kind, slot], precv.at[kind, slot], req=mate)

    def compute(plane):
        remote(late(plane, 1 - x), late(plane, 1 - x), qsend.at[4, plane], qrecv.at[2, plane], req=mate).wait_recv()
        far = cached(plane * 2 + 1 - x)
        save(plane, 0, far[:1])
        over[0, plane] = pack_partial(far[1:])
        send_over(plane).start()
        save(plane, 1, cached(plane * 2 + x))

    def finish(way, plane, has_source):
        def pass_on(buffer, kind, partial):
            if has_source:
                arriving(buffer, kind, plane).wait_recv()
                partial = merge(partial, unpack_partial(buffer[plane]))
            buffer[plane] = pack_partial(partial)
            passing(buffer, kind, way, plane).start()

        pass_on(first_way, 0, load(plane, 0, 2))
        send_over(plane).wait_recv()
        pass_on(rest_way, 1, merge(load(plane, 2, 5), unpack_partial(over[1, plane])))

    def return_step(step, carry):
        high = z + 1 + step
        low = z - 1 - step
        starts_up = jnp.logical_or(z == 0, jnp.logical_and(z == 1, high == nz - 1))
        starts_down = jnp.logical_or(z == nz - 1, jnp.logical_and(z == nz - 2, low == 0))
        pl.when(high < nz)(lambda: compute(high))
        pl.when(jnp.logical_and(high < nz, starts_up))(lambda: finish(0, high, False))
        relay(step + 1)
        pl.when(low >= 0)(lambda: compute(low))
        pl.when(jnp.logical_and(low >= 0, starts_down))(lambda: finish(1, low, False))
        return carry

    loads[0].wait()
    wo_y = remote(wo_all.at[tp], wo_all.at[tp], tsend.at[0], trecv.at[0], tp=y_mate)
    wo_core = remote(wo_all.at[tp], wo_all.at[tp], tsend.at[1], trecv.at[1], tp=core_mate)
    wo_y.start()
    wo_core.start()
    lax.fori_loop(0, nz - 1, return_step, 0)
    def merge_step(step, carry):
        distance = nz - 3 - step
        high = z + distance
        low = z - distance
        pl.when(jnp.logical_and(high < nz, not_first))(lambda: finish(0, high, True))
        pl.when(jnp.logical_and(low >= 0, not_last))(lambda: finish(1, low, True))
        return carry

    lax.fori_loop(0, nz - 3, merge_step, 0)
    far = cached(mate)
    save(z, 0, far[:1])
    over[0, z] = pack_partial(far[1:])
    send_over(z).start()
    save(z, 1, merge(load(z, 1, 5), cached(me)))

    def gather_in(buffer, kind, slot, held):
        arriving(buffer, kind, slot).wait_recv()
        return merge(held, unpack_partial(buffer[slot]))

    firsts = load(z, 0, 2)
    firsts = gather_in(first_way, 0, z, firsts)
    firsts = gather_in(first_way, 0, nz, firsts)
    cross[0] = pack_partial(firsts[:1])
    to_mate = remote(cross.at[0], cross.at[1], xsend, xrecv, req=mate)
    to_mate.start()

    remote(wo_all.at[y_mate], wo_all.at[y_mate], tsend.at[0], trecv.at[0], tp=y_mate).wait_recv()
    wo_far = remote(wo_all.at[y_mate], wo_all.at[y_mate], tsend.at[2], trecv.at[2], tp=core_mate)
    wo_far.start()

    loads[3].wait()
    down_t[...] = down_v[...].T
    send_over(z).wait_recv()
    rest = merge(load(z, 2, 5), unpack_partial(over[1, z]))
    rest = gather_in(rest_way, 1, z, rest)
    rest = gather_in(rest_way, 1, nz, rest)
    to_mate.wait_recv()
    mine = merge(firsts[1:], unpack_partial(cross[1])) + rest
    att[tp] = jnp.concatenate([(numer / total).astype(BF16) for numer, _, total in mine], axis=0)

    att_y = remote(att.at[tp], att.at[tp], tsend.at[3], trecv.at[3], tp=y_mate)
    att_core = remote(att.at[tp], att.at[tp], tsend.at[4], trecv.at[4], tp=core_mate)
    att_y.start()
    att_core.start()

    def projected(index):
        return matmul(att[index].T, wo_all[index])

    terms = projected(tp)
    remote(wo_all.at[core_mate], wo_all.at[core_mate], tsend.at[1], trecv.at[1], tp=core_mate).wait_recv()
    remote(att.at[core_mate], att.at[core_mate], tsend.at[4], trecv.at[4], tp=core_mate).wait_recv()
    terms = terms + projected(core_mate)
    remote(att.at[y_mate], att.at[y_mate], tsend.at[3], trecv.at[3], tp=y_mate).wait_recv()
    att_far = remote(att.at[y_mate], att.at[y_mate], tsend.at[5], trecv.at[5], tp=core_mate)
    att_far.start()
    terms = terms + projected(y_mate)
    diagonal = (core_mate + 2) % 4
    remote(wo_all.at[diagonal], wo_all.at[diagonal], tsend.at[2], trecv.at[2], tp=core_mate).wait_recv()
    remote(att.at[diagonal], att.at[diagonal], tsend.at[5], trecv.at[5], tp=core_mate).wait_recv()
    terms = terms + projected(diagonal)

    middle = (tokens[...].astype(F32) + terms).astype(BF16).astype(F32)
    normed_middle = normalize(middle, gain_f[...].astype(F32)[None, :])
    loads[4].wait()
    gate = matmul_rows(up_v[...], normed_middle)
    hidden_t = (gate / (1.0 + jnp.exp(-gate))).astype(BF16)

    def down_part(index):
        return matmul(down_t[pl.ds(pl.multiple_of(index * WIDTH, 16), WIDTH)], hidden_t)

    core_out[0] = down_part(diagonal).astype(BF16)
    fold = remote(core_out.at[0], core_in.at[0], tsend.at[6], trecv.at[6], tp=core_mate)
    fold.start()
    far_part = down_part(y_mate)
    core_out[1] = down_part(core_mate).astype(BF16)
    fold_near = remote(core_out.at[1], core_in.at[1], tsend.at[8], trecv.at[8], tp=core_mate)
    fold_near.start()
    fold.wait_recv()
    y_out[...] = (far_part + core_in[0].astype(F32)).astype(BF16)
    swap = remote(y_out, y_in, tsend.at[7], trecv.at[7], tp=y_mate)
    swap.start()
    near_part = down_part(tp)
    mid_t[...] = middle.T
    near_part = near_part + mid_t[pl.ds(pl.multiple_of(tp * WIDTH, 16), WIDTH)]
    fold_near.wait_recv()
    near_part = near_part + core_in[1].astype(F32)
    lane = lax.broadcasted_iota(jnp.int32, (WIDTH, ROWS), 1)
    live = jnp.where(lane < SLOT, length[me * R_DEV], length[me * R_DEV + 1])
    swap.wait_recv()
    layer = near_part + y_in[...].astype(F32)
    out[...] = jnp.where(lane % SLOT < live, layer, 0.0).astype(BF16)

    over_whole.wait_send()

    def sent_step(plane, carry):
        pl.when(plane != z)(lambda: over_late(plane).wait_send())

        @pl.when(jnp.logical_and(not_last, plane <= z))
        def _():
            up_whole(plane).wait_send()
            up_early(plane).wait_send()

        @pl.when(jnp.logical_and(not_first, plane >= z))
        def _():
            down_whole(plane).wait_send()
            down_early(plane).wait_send()

        send_over(plane).wait_send()

        for kind, buffer in ((0, first_way), (1, rest_way)):
            pl.when(plane > z)(lambda: passing(buffer, kind, 0, plane).wait_send())
            pl.when(plane < z)(lambda: passing(buffer, kind, 1, plane).wait_send())

        return carry

    lax.fori_loop(0, nz, sent_step, 0)
    for copy in (to_mate, wo_y, wo_core, wo_far, att_y, att_core, att_far, fold, fold_near, swap):
        copy.wait_send()


def per_device(
    tokens,
    attention_gain,
    feedforward_gain,
    query_weight,
    key_weight,
    value_weight,
    out_weight,
    up_weight,
    down_weight,
    cache_keys,
    cache_values,
    request_prefix,
    suffix_length,
):
    owners = lax.axis_size("req")
    nz = owners // 2
    rows, model = tokens.shape
    prefixes = cache_keys.shape[1]
    dma = pltpu.SemaphoreType.DMA
    vmem = pl.BlockSpec(memory_space=pltpu.VMEM)
    smem = pl.BlockSpec(memory_space=pltpu.SMEM)
    away = pl.BlockSpec(memory_space=pl.ANY)
    return pl.pallas_call(
        functools.partial(kernel, nz),
        out_shape=jax.ShapeDtypeStruct((WIDTH, rows), BF16),
        in_specs=[vmem] * 4 + [away] * 7 + [smem] * 2,
        out_specs=vmem,
        scratch_shapes=[
            pltpu.VMEM((owners, WIDTH, ROWS), BF16),
            pltpu.VMEM((prefixes, PG, WIDTH), BF16),
            pltpu.VMEM((prefixes, PG, WIDTH), BF16),
            pltpu.VMEM((4, WIDTH, model), BF16),
            pltpu.VMEM((WIDTH, model), BF16),
            pltpu.VMEM((WIDTH, model), BF16),
            pltpu.VMEM((model, WIDTH), BF16),
            pltpu.VMEM((ROWS, WIDTH), BF16),
            pltpu.VMEM((WIDTH, ROWS), BF16),
            pltpu.VMEM((prefixes, WIDTH, PG), BF16),
            pltpu.VMEM((nz, FIRST + WIDTH, ROWS), F32),
            pltpu.VMEM((nz, STATS, ROWS), F32),
            pltpu.VMEM((nz + 1, REST + STATS, ROWS), BF16),
            pltpu.VMEM((nz + 1, 2 * FIRST + STATS, ROWS), BF16),
            pltpu.VMEM((2, nz, REST + STATS, ROWS), BF16),
            pltpu.VMEM((2, FIRST + STATS, ROWS), BF16),
            pltpu.VMEM((4, WIDTH, ROWS), BF16),
            pltpu.VMEM((2, WIDTH, ROWS), BF16),
            pltpu.VMEM((2, WIDTH, ROWS), BF16),
            pltpu.VMEM((WIDTH, ROWS), BF16),
            pltpu.VMEM((WIDTH, ROWS), BF16),
            pltpu.VMEM((model, ROWS), F32),
            dma((7,)),
            dma((5, nz)),
            dma((3, nz)),
            dma((2, nz + 1)),
            dma((2, nz + 1)),
            dma,
            dma,
            dma((9,)),
            dma((9,)),
            dma((nz,)),
            dma((nz,)),
            pltpu.VMEM((WIDTH, model), BF16),
            pltpu.VMEM((WIDTH, model), BF16),
        ],
        compiler_params=pltpu.CompilerParams(
            collective_id=0, has_side_effects=True, vmem_limit_bytes=60 * 1024 * 1024
        ),
    )(
        tokens,
        attention_gain,
        feedforward_gain,
        query_weight.T,
        key_weight.T,
        value_weight.T,
        out_weight,
        up_weight.T,
        down_weight,
        cache_keys[0],
        cache_values[0],
        request_prefix,
        suffix_length,
    ).T


def solution(mesh):
    in_specs = (
        P("req", None),
        P(),
        P(),
        P(None, "tp"),
        P(None, "tp"),
        P(None, "tp"),
        P("tp", None),
        P(None, "tp"),
        P("tp", None),
        P("req", None, None, "tp"),
        P("req", None, None, "tp"),
        P(),
        P(),
    )
    out_specs = P("req", "tp")
    return jax.shard_map(
        per_device, mesh=mesh, in_specs=in_specs, out_specs=out_specs, check_vma=False
    )
```
